512 devices in a mesh: head: 16 (over x_hi, z), seq: 32 (over x_lo, y, core).
Axes of the slice: x: 4 (x_hi: 2, x_lo: 2; x = x_hi * 2 + x_lo), y: 8, z: 8, core: 2. Of those that a mesh axis runs over, the one named last changes fastest.
Arguments:
- context: bfloat16 [1536, 14336], P('head', 'seq'), may hold values from -6 to 6
- stream: bfloat16 [1536, 14336], P('head', 'seq'), may hold values from -16 to 16
- out_weight: bfloat16 [1536, 1536], P('head'), may hold values from -0.21875 to 0.21875
- ln_gain: float32 [1536], replicated, may hold values from 0.1 to 1.9
- ln_bias: float32 [1536], replicated, may hold values from -3 to 3
- glu_weight: bfloat16 [2, 1536, 1536], P(None, 'head'), may hold values from -0.15625 to 0.15625
- depth_kernel: float32 [1536, 31], P('head'), may hold values from -1 to 1
- bn_gain: float32 [1536], P('head'), may hold values from 0.1 to 1.9
- bn_bias: float32 [1536], P('head'), may hold values from -3 to 3
- proj_weight: bfloat16 [1536, 1536], P('head'), may hold values from -0.21875 to 0.21875
- out_grad: bfloat16 [1536, 14336], P('head', 'seq'), may hold values from -6 to 6
Outputs:
- output: bfloat16 [1536, 14336], P('head', 'seq')
- stream_grad: bfloat16 [1536, 14336], P('head', 'seq')
- context_grad: bfloat16 [1536, 14336], P('head', 'seq')
- out_weight_grad: float32 [1536, 1536], P('head')
- glu_weight_grad: float32 [2, 1536, 1536], P(None, 'head')
- kernel_grad: float32 [1536, 31], P('head')
- bn_gain_grad: float32 [1536], P('head')
- bn_bias_grad: float32 [1536], P('head')
- proj_weight_grad: float32 [1536, 1536], P('head')
The draws below stay inside these ranges and needn't reach their ends.
All inputs are finite; a program needn't handle non-finite values.
Results may differ from the reference program's by a relative error of at most 0.03.
Values may be sent and summed in bfloat16 or wider, within the bound.
No kernel may reach another device: no remote copies, remote signals or barrier semaphores. Data moves between devices by JAX's collectives and lax.ppermute only.
A program may use at most 64 MiB of HBM per device.

```python
import jax
import jax.numpy as jnp
from jax import lax

D = 1536
KERNEL = 31
HD = 1536
FRAMES = 14336
N_HEAD = 16


def draw_stream(key, part):
    key = jax.random.fold_in(key, 11)
    key_noise, key_common, key_column = jax.random.split(key, 3)
    channel = jnp.arange(D, dtype=jnp.float32)[:, None]
    frame = jnp.arange(FRAMES, dtype=jnp.float32)[None, :]
    ramp = frame / FRAMES
    common = jnp.clip(jax.random.normal(key_common, (D, 1), jnp.float32), -3.0, 3.0)
    column = jnp.exp(jax.random.uniform(key_column, (1, FRAMES), jnp.float32, -0.7, 0.7))
    chan_scale = jnp.exp(jnp.log(3.0) * channel / D)
    noise = jnp.clip(jax.random.normal(key_noise, (D, FRAMES), jnp.float32), -3.0, 3.0)
    result = 0.3 * (noise * column + ramp * common) * chan_scale
    return result.astype(jnp.bfloat16)


def spiked(array, rng, source, target, parts, factor):
    owner, partner = [(jnp.arange(array.shape[dim]) // (array.shape[dim] // parts)).reshape([-1 if axis == dim else 1 for axis in range(array.ndim)]) for dim in (source, target)]
    chosen = jax.random.permutation(rng, parts)[partner]
    strong = (owner == chosen) | (owner == (partner + parts // 2) % parts)
    return jnp.where(strong, factor * array, array)


def block_scale(own_key, extent, cuts, least, largest):
    factor_of = 1.0
    for dim, shards_of in cuts:
        steps = jax.random.uniform(jax.random.fold_in(jax.random.fold_in(own_key, 6), dim), (shards_of,), jnp.float32, least / len(cuts), largest / len(cuts))
        factor_of = factor_of * jnp.repeat(jnp.exp(steps), extent[dim] // shards_of).reshape((-1,) + (1,) * (len(extent) - 1 - dim))
    return factor_of


def gaussian(stream_key, dims, width, most, cuts=(), held_as=jnp.bfloat16):
    level = block_scale(stream_key, dims, cuts, -0.22, 0.18) if cuts else 1.0
    drawn = jax.random.normal(stream_key, dims, jnp.float32) * width * level
    return jnp.minimum(jnp.maximum(drawn, -most), most).astype(held_as)


def heavy_noise(rng, dims, scale, bound, pieces, heavy, kind=jnp.bfloat16):
    values = scale * jax.random.normal(rng, dims, jnp.float32)
    if pieces:
        values = values * block_scale(rng, dims, pieces, -0.22, 0.18)
    return jnp.clip(spiked(values, jax.random.fold_in(rng, 3), *heavy), -bound, bound).astype(kind)


def setup_inputs(seed: int = 0) -> dict:
    arg_keys = jax.random.split(jax.random.key(seed), 12)
    context = gaussian(arg_keys[0], (HD, FRAMES), 1.0, 6.0, ((0, 16), (1, 32)))
    stream = draw_stream(jax.random.fold_in(arg_keys[11], 71), 0)
    out_weight = heavy_noise(arg_keys[2], (HD, D), HD ** -0.5, 0.21875, ((0, 16),), (0, 1, 16, 2.0))
    ln_gain = jnp.clip(1.0 + 0.18 * jax.random.normal(arg_keys[3], (D,), jnp.float32), 0.1, 1.9)
    ln_bias = gaussian(arg_keys[4], (D,), 0.5, 3.0, (), jnp.float32)
    glu_weight = gaussian(arg_keys[5], (2, D, D), D ** -0.5, 0.15625, ((1, 16),))
    depth_kernel = gaussian(arg_keys[6], (D, KERNEL), KERNEL ** -0.5, 1.0, ((0, 16),), jnp.float32)
    bn_gain = jnp.clip(1.0 + 0.18 * jax.random.normal(arg_keys[7], (D,), jnp.float32), 0.1, 1.9)
    bn_bias = gaussian(arg_keys[8], (D,), 0.5, 3.0, ((0, 16),), jnp.float32)
    proj_weight = heavy_noise(arg_keys[9], (D, D), D ** -0.5, 0.21875, ((0, 16),), (0, 1, 16, 2.0))
    out_grad = gaussian(arg_keys[10], (D, FRAMES), 1.0, 6.0, ((0, 16), (1, 32)))
    return {"context": context, "stream": stream, "out_weight": out_weight, "ln_gain": ln_gain, "ln_bias": ln_bias, "glu_weight": glu_weight, "depth_kernel": depth_kernel, "bn_gain": bn_gain, "bn_bias": bn_bias, "proj_weight": proj_weight, "out_grad": out_grad}


epsilon = 1e-05

def round_half(values_in):
    narrow = values_in.astype(jnp.bfloat16)
    narrow = lax.optimization_barrier(narrow)
    return narrow.astype(jnp.float32)

def grouped_sum(weight_groups, operand_groups):

    def add_group(running, group_pair):
        partial_term = lax.dot_general(group_pair[0], group_pair[1], (((0,), (0,)), ((), ())), preferred_element_type=jnp.float32)
        return (running + round_half(partial_term), None)
    initial = jnp.zeros((weight_groups.shape[2], operand_groups.shape[2]), jnp.float32)
    running, unused = lax.scan(add_group, initial, (weight_groups, operand_groups))
    return running

def split_rows(values_in):
    return values_in.reshape(N_HEAD, values_in.shape[0] // N_HEAD, values_in.shape[1])

def split_pairs(values_in):
    per_group = values_in.shape[1] // N_HEAD
    grouped = values_in.reshape(2, N_HEAD, per_group, values_in.shape[2])
    return jnp.transpose(grouped, (1, 0, 2, 3)).reshape(N_HEAD, 2 * per_group, values_in.shape[2])

def reference(context, stream, out_weight, ln_gain, ln_bias, glu_weight, depth_kernel, bn_gain, bn_bias, proj_weight, out_grad):
    frames_all = stream.shape[1]
    kernel_width = depth_kernel.shape[1]
    half_width = kernel_width // 2
    attention = grouped_sum(split_rows(out_weight), split_rows(context))
    hidden = (stream.astype(jnp.float32) + attention).astype(jnp.bfloat16)
    residual = hidden.astype(jnp.float32)
    frame_mean = lax.optimization_barrier(jnp.mean(residual, axis=0, keepdims=True))
    centered = residual - frame_mean
    frame_rstd = lax.rsqrt(lax.optimization_barrier(jnp.mean(centered * centered, axis=0, keepdims=True)) + epsilon)
    standard = centered * frame_rstd
    normed = (standard * ln_gain[:, None] + ln_bias[:, None]).astype(jnp.bfloat16)
    glu_value = jnp.dot(glu_weight[0], normed, preferred_element_type=jnp.float32)
    glu_gate = jnp.dot(glu_weight[1], normed, preferred_element_type=jnp.float32)
    gate_sig = jax.nn.sigmoid(glu_gate)
    gated_out = (glu_value * gate_sig).astype(jnp.bfloat16)
    padded = jnp.pad(gated_out.astype(jnp.float32), ((0, 0), (half_width, half_width)))
    conv_out = depth_kernel[:, 0:1] * padded[:, 0:frames_all]
    for tap_index in range(1, kernel_width):
        conv_out = conv_out + depth_kernel[:, tap_index:tap_index + 1] * padded[:, tap_index:tap_index + frames_all]
    chan_mean = lax.optimization_barrier(jnp.mean(conv_out, axis=1, keepdims=True))
    chan_cent = conv_out - chan_mean
    chan_rstd = lax.rsqrt(lax.optimization_barrier(jnp.mean(chan_cent * chan_cent, axis=1, keepdims=True)) + epsilon)
    chan_unit = chan_cent * chan_rstd
    shifted = chan_unit * bn_gain[:, None] + bn_bias[:, None]
    shift_sig = jax.nn.sigmoid(shifted)
    swished = (shifted * shift_sig).astype(jnp.bfloat16)
    branch = grouped_sum(split_rows(proj_weight), split_rows(swished))
    output = (residual + branch).astype(jnp.bfloat16)
    swish_grad = jnp.dot(proj_weight, out_grad, preferred_element_type=jnp.float32)
    proj_weight_grad = lax.dot_general(swished, out_grad, (((1,), (1,)), ((), ())), preferred_element_type=jnp.float32)
    shift_grad = swish_grad * shift_sig * (1.0 + shifted * (1.0 - shift_sig))
    bn_bias_grad = lax.optimization_barrier(jnp.sum(shift_grad, axis=1))
    bn_gain_grad = lax.optimization_barrier(jnp.sum(shift_grad * chan_unit, axis=1))
    conv_grad = (chan_rstd * bn_gain[:, None] * (shift_grad - bn_bias_grad[:, None] / frames_all - chan_unit * bn_gain_grad[:, None] / frames_all)).astype(jnp.bfloat16)
    conv_float = conv_grad.astype(jnp.float32)
    grad_wide = jnp.pad(conv_float, ((0, 0), (half_width, half_width)))
    gated_grad = depth_kernel[:, 0:1] * grad_wide[:, 2 * half_width:2 * half_width + frames_all]
    kernel_cols = [lax.optimization_barrier(jnp.sum(conv_float * padded[:, 0:frames_all], axis=1))]
    for tap_index in range(1, kernel_width):
        back_index = 2 * half_width - tap_index
        gated_grad = gated_grad + depth_kernel[:, tap_index:tap_index + 1] * grad_wide[:, back_index:back_index + frames_all]
        kernel_cols.append(lax.optimization_barrier(jnp.sum(conv_float * padded[:, tap_index:tap_index + frames_all], axis=1)))
    kernel_grad = jnp.stack(kernel_cols, axis=1)
    pair_grad = jnp.stack([gated_grad * gate_sig, gated_grad * glu_value * gate_sig * (1.0 - gate_sig)]).astype(jnp.bfloat16)
    glu_weight_grad = jnp.einsum('jct,dt->jcd', pair_grad.astype(jnp.float32), normed.astype(jnp.float32))
    normed_grad = grouped_sum(split_pairs(glu_weight), split_pairs(pair_grad))
    scaled = normed_grad * ln_gain[:, None]
    full_grad = out_grad.astype(jnp.float32) + frame_rstd * (scaled - lax.optimization_barrier(jnp.mean(scaled, axis=0, keepdims=True)) - standard * lax.optimization_barrier(jnp.mean(scaled * standard, axis=0, keepdims=True)))
    stream_grad = full_grad.astype(jnp.bfloat16)
    context_grad = jnp.dot(out_weight, stream_grad, preferred_element_type=jnp.float32).astype(jnp.bfloat16)
    out_weight_grad = lax.dot_general(context, stream_grad, (((1,), (1,)), ((), ())), preferred_element_type=jnp.float32)
    return (output, stream_grad, context_grad, out_weight_grad, glu_weight_grad, kernel_grad, bn_gain_grad, bn_bias_grad, proj_weight_grad)
```

```python
import jax
import jax.numpy as jnp
from jax import lax
from jax.sharding import PartitionSpec as P

epsilon = 1e-05
f32 = jnp.float32
bf16 = jnp.bfloat16


def contract_lead(first_op, second_op):
    return lax.dot_general(
        first_op, second_op, (((0,), (0,)), ((), ())), preferred_element_type=f32
    )


def contract_last(first_op, second_op):
    return lax.dot_general(
        first_op, second_op, (((1,), (1,)), ((), ())), preferred_element_type=f32
    )


def exchange(blocks, axis):
    return lax.all_to_all(blocks, axis, 0, 0, tiled=True)


def gather(block, axis):
    count = lax.axis_size(axis)
    copies = jnp.broadcast_to(block[None], (count, *block.shape))
    return exchange(copies, axis)


def neighbours(operand, half_width):
    count, length = lax.axis_size("seq"), operand.shape[1]
    up = [(i, (i + 1) % count) for i in range(count - 1)]
    down = [(j, i) for i, j in up]
    before = lax.ppermute(operand[:, length - half_width :], "seq", up)
    after = lax.ppermute(operand[:, :half_width], "seq", down)
    return jnp.concatenate([before, operand, after], axis=1)


def on_device(
    context,
    stream,
    out_weight,
    ln_gain,
    ln_bias,
    glu_weight,
    depth_kernel,
    bn_gain,
    bn_bias,
    proj_weight,
    out_grad,
):
    rows, frames = stream.shape
    width = ln_gain.shape[0]
    heads = lax.axis_size("head")
    parts = lax.axis_size("seq")
    frames_all = frames * parts
    taps = depth_kernel.shape[1]
    half = taps // 2
    me = lax.axis_index("head")
    gain_col = ln_gain[:, None]
    bias_col = ln_bias[:, None]

    att_part = contract_lead(out_weight, context).astype(bf16).reshape(heads, rows, frames)
    attention = jnp.sum(exchange(att_part, "head").astype(f32), axis=0)
    hidden = (stream.astype(f32) + attention).astype(bf16)

    hidden_full = gather(hidden, "head").reshape(width, frames)
    grad_full = lax.all_gather(out_grad, "head", axis=0, tiled=True)
    hidden_full, grad_full = lax.optimization_barrier((hidden_full, grad_full))
    wide = hidden_full.astype(f32)
    centered = wide - jnp.mean(wide, axis=0, keepdims=True)
    frame_rstd = lax.rsqrt(jnp.mean(centered * centered, axis=0, keepdims=True) + epsilon)
    standard = centered * frame_rstd
    normed = (standard * gain_col + bias_col).astype(bf16)

    pair_out = jnp.einsum("jcd,dt->jct", glu_weight, normed, preferred_element_type=f32)
    glu_value, glu_gate = pair_out[0], pair_out[1]
    gate_sig = jax.nn.sigmoid(glu_gate)
    gated_out = (glu_value * gate_sig).astype(bf16)
    widened = neighbours(gated_out, half).astype(f32)
    conv_out = depth_kernel[:, 0:1] * widened[:, 0:frames]
    for tap in range(1, taps):
        conv_out = conv_out + depth_kernel[:, tap : tap + 1] * widened[:, tap : tap + frames]

    block_mean = jnp.mean(conv_out, axis=1)
    block_cent = conv_out - block_mean[:, None]
    block_square = jnp.sum(block_cent * block_cent, axis=1)
    moments = gather(jnp.stack([block_mean, block_square]), "seq")
    chan_mean = jnp.mean(moments[:, 0], axis=0)
    mean_gap = moments[:, 0] - chan_mean
    chan_var = (
        jnp.sum(moments[:, 1], axis=0) + frames * jnp.sum(mean_gap * mean_gap, axis=0)
    ) / frames_all
    chan_rstd = lax.rsqrt(chan_var + epsilon)[:, None]
    chan_unit = (conv_out - chan_mean[:, None]) * chan_rstd
    shifted = chan_unit * bn_gain[:, None] + bn_bias[:, None]
    shift_sig = jax.nn.sigmoid(shifted)
    swished = (shifted * shift_sig).astype(bf16)

    swish_grad = jnp.dot(proj_weight, grad_full, preferred_element_type=f32)
    shift_grad = swish_grad * shift_sig * (1.0 + shifted * (1.0 - shift_sig))
    sums = gather(
        jnp.stack([jnp.sum(shift_grad, axis=1), jnp.sum(shift_grad * chan_unit, axis=1)]), "seq"
    )
    bias_total, gain_total = jnp.sum(sums[:, 0], axis=0), jnp.sum(sums[:, 1], axis=0)
    conv_grad = (
        chan_rstd
        * bn_gain[:, None]
        * (
            shift_grad
            - (bias_total / frames_all)[:, None]
            - chan_unit * (gain_total / frames_all)[:, None]
        )
    ).astype(bf16)
    conv_float = conv_grad.astype(f32)
    grad_wide = neighbours(conv_grad, half).astype(f32)
    gated_grad = depth_kernel[:, 0:1] * grad_wide[:, 2 * half : 2 * half + frames]
    kernel_cols = [jnp.sum(conv_float * widened[:, 0:frames], axis=1)]
    for tap in range(1, taps):
        back = 2 * half - tap
        gated_grad = (
            gated_grad + depth_kernel[:, tap : tap + 1] * grad_wide[:, back : back + frames]
        )
        kernel_cols.append(jnp.sum(conv_float * widened[:, tap : tap + frames], axis=1))
    kernel_part = jnp.stack(kernel_cols, axis=1)
    pair_grad = jnp.stack(
        [gated_grad * gate_sig, gated_grad * glu_value * gate_sig * (1.0 - gate_sig)]
    ).astype(bf16)

    branch_part = contract_lead(proj_weight, swished).astype(bf16)
    normed_part = jnp.einsum(
        "jcd,jct->dt", glu_weight, pair_grad, preferred_element_type=f32
    ).astype(bf16)
    both = jnp.stack(
        [branch_part.reshape(heads, rows, frames), normed_part.reshape(heads, rows, frames)],
        axis=1,
    )
    both = jnp.sum(exchange(both, "head").astype(f32), axis=0)
    output = (hidden.astype(f32) + both[0]).astype(bf16)

    normed_grad = gather(both[1].astype(bf16), "head").reshape(width, frames).astype(f32)
    scaled = normed_grad * gain_col
    stream_full = (
        grad_full.astype(f32)
        + frame_rstd
        * (
            scaled
            - jnp.mean(scaled, axis=0, keepdims=True)
            - standard * jnp.mean(scaled * standard, axis=0, keepdims=True)
        )
    ).astype(bf16)
    stream_grad = lax.dynamic_slice_in_dim(stream_full, me * rows, rows)
    context_grad = jnp.dot(out_weight, stream_full, preferred_element_type=f32).astype(bf16)

    proj_part = contract_last(swished, grad_full)
    glu_part = jnp.einsum("jct,dt->jcd", pair_grad, normed, preferred_element_type=f32)
    out_part = contract_last(context, stream_full)
    stacked = jnp.concatenate([proj_part[None], glu_part, out_part[None]]).astype(bf16)
    pieces = stacked.reshape(parts, -1, 1152)
    piece = jnp.sum(exchange(pieces, "seq").astype(f32), axis=0)
    totals = gather(piece.astype(bf16), "seq").reshape(4, rows, width).astype(f32)
    kernel_grad = jnp.sum(gather(kernel_part, "seq"), axis=0)
    return (
        output,
        stream_grad,
        context_grad,
        totals[3],
        totals[1:3],
        kernel_grad,
        gain_total,
        bias_total,
        totals[0],
    )


def solution(mesh):
    return jax.shard_map(
        on_device,
        mesh=mesh,
        in_specs=(
            P("head", "seq"),
            P("head", "seq"),
            P("head", None),
            P(),
            P(),
            P(None, "head", None),
            P("head", None),
            P("head"),
            P("head"),
            P("head", None),
            P("head", "seq"),
        ),
        out_specs=(
            P("head", "seq"),
            P("head", "seq"),
            P("head", "seq"),
            P("head", None),
            P(None, "head", None),
            P("head", None),
            P("head"),
            P("head"),
            P("head", None),
        ),
        check_vma=False,
    )
```

```python
import functools

import jax
import jax.numpy as jnp
from jax import lax
from jax.experimental import pallas as pl
from jax.experimental.pallas import tpu as pltpu
from jax.sharding import PartitionSpec as P

epsilon = 1e-05
f32 = jnp.float32
bf16 = jnp.bfloat16


def contract_lead(first_op, second_op):
    return lax.dot_general(
        first_op, second_op, (((0,), (0,)), ((), ())), preferred_element_type=f32
    )


def contract_last(first_op, second_op):
    return lax.dot_general(
        first_op, second_op, (((1,), (1,)), ((), ())), preferred_element_type=f32
    )


def exchange(blocks, axis):
    return lax.all_to_all(blocks, axis, 0, 0, tiled=True)


def gather(block, axis):
    count = lax.axis_size(axis)
    copies = jnp.broadcast_to(block[None], (count, *block.shape))
    return exchange(copies, axis)


def line_groups():
    half = lax.axis_size("head") // 2
    return [[side * half + i for i in range(half)] for side in range(2)]


def across(operand):
    count = lax.axis_size("head")
    return lax.ppermute(operand, "head", [(i, (i + count // 2) % count) for i in range(count)])


def swap_bit(operand, bit):
    count = lax.axis_size("seq")
    return lax.ppermute(operand, "seq", [(i, i ^ bit) for i in range(count)])


def halves(operand, bit):
    mine = (lax.axis_index("seq") // bit) % 2
    size = operand.shape[0] // 2
    keep = lax.dynamic_slice_in_dim(operand, mine * size, size)
    send = lax.dynamic_slice_in_dim(operand, (1 - mine) * size, size)
    return keep, send


def joined(mine_rows, other_rows, bit):
    low = (lax.axis_index("seq") // bit) % 2 == 0
    return jnp.concatenate(
        [jnp.where(low, mine_rows, other_rows), jnp.where(low, other_rows, mine_rows)]
    )


def shifted_left(operand, distance):
    lanes = operand.shape[1]
    return pltpu.roll(operand, (lanes - distance) % lanes, 1)


def conv_back_kernel(
    consts_ref, taps_ref, inside_ref, swish_ref, conv_ref, pair_out_ref, pair_ref, grad_ref, *, taps
):
    frames = pair_ref.shape[2]

    def chunk(index, carry):
        at = pl.ds(pl.multiple_of(index * 16, 16), 16)
        consts = consts_ref[at, :]
        mean, rstd, gain, bias = (consts[:, i : i + 1] for i in range(4))
        bias_mean, gain_mean = consts[:, 4:5], consts[:, 5:6]
        unit = (conv_ref[at, :] - mean) * rstd
        shifted = unit * gain + bias
        sig = jax.nn.sigmoid(shifted)
        shift_grad = swish_ref[at, :] * sig * (1.0 + shifted * (1.0 - sig))
        grad = rstd * gain * (shift_grad - bias_mean - unit * gain_mean)
        grad = jnp.where(inside_ref[...] > 0.0, grad, 0.0).astype(bf16).astype(f32)
        grad_ref[at, :] = grad
        kernel = taps_ref[at, :]
        total = kernel[:, 0:1] * shifted_left(grad, taps - 1)[:, :frames]
        for tap in range(1, taps):
            total = total + kernel[:, tap : tap + 1] * shifted_left(grad, taps - 1 - tap)[:, :frames]
        gate_sig = jax.nn.sigmoid(pair_out_ref[1, at, :])
        value_grad = total * gate_sig
        pair_ref[0, at, :] = value_grad.astype(bf16)
        pair_ref[1, at, :] = (value_grad * pair_out_ref[0, at, :] * (1.0 - gate_sig)).astype(bf16)
        return carry

    lax.fori_loop(0, pair_ref.shape[1] // 16, chunk, 0)


def taps_grad_kernel(grad_ref, widened_ref, out_ref, *, taps, frames):
    half = taps // 2
    column = lax.broadcasted_iota(jnp.int32, (16, out_ref.shape[1]), 1)

    def chunk(index, carry):
        at = pl.ds(pl.multiple_of(index * 16, 16), 16)
        grad = shifted_left(grad_ref[at, :], half)[:, :frames]
        widened = widened_ref[at, :]
        out = jnp.zeros(column.shape, f32)
        for tap in range(taps):
            near = shifted_left(widened, half + tap)[:, :frames]
            out = jnp.where(column == tap, jnp.sum(grad * near, axis=1, keepdims=True), out)
        out_ref[at, :] = out
        return carry

    lax.fori_loop(0, out_ref.shape[0] // 16, chunk, 0)


def conv_back(consts, kernel, inside, swish_wide, conv_wide, pair_out, taps):
    return pl.pallas_call(
        functools.partial(conv_back_kernel, taps=taps),
        out_shape=(
            jax.ShapeDtypeStruct(pair_out.shape, bf16),
            jax.ShapeDtypeStruct(conv_wide.shape, f32),
        ),
        name="conv_back",
    )(consts, kernel, inside, swish_wide, conv_wide, pair_out)


def taps_grad(grad_wide, widened, taps, frames):
    return pl.pallas_call(
        functools.partial(taps_grad_kernel, taps=taps, frames=frames),
        out_shape=jax.ShapeDtypeStruct((grad_wide.shape[0], 128), f32),
        name="taps_grad",
    )(grad_wide, widened)


def neighbours(operand, half_width, lanes):
    count, length = lax.axis_size("seq"), operand.shape[1]
    up = [(i, (i + 1) % count) for i in range(count - 1)]
    down = [(j, i) for i, j in up]
    before = lax.ppermute(operand[:, length - half_width :], "seq", up)
    after = lax.ppermute(operand[:, :half_width], "seq", down)
    spare = jnp.zeros((operand.shape[0], lanes - length - 2 * half_width), operand.dtype)
    return jnp.concatenate([before, operand, after, spare], axis=1)


def on_device(
    context,
    stream,
    out_weight,
    ln_gain,
    ln_bias,
    glu_weight,
    depth_kernel,
    bn_gain,
    bn_bias,
    proj_weight,
    out_grad,
):
    rows, frames = stream.shape
    width = ln_gain.shape[0]
    heads = lax.axis_size("head")
    parts = lax.axis_size("seq")
    frames_all = frames * parts
    taps = depth_kernel.shape[1]
    half = taps // 2
    lanes = -(-(frames + 4 * half) // 128) * 128
    me = lax.axis_index("head")
    line = heads // 2
    side = me // line
    gain_col = ln_gain[:, None]
    bias_col = ln_bias[:, None]

    def own_half(weight):
        keep = lax.dynamic_slice_in_dim(weight, side * (width // 2), width // 2, axis=1)
        send = lax.dynamic_slice_in_dim(weight, (1 - side) * (width // 2), width // 2, axis=1)
        return keep, across(send)

    def line_exchange(blocks):
        blocks = lax.all_to_all(
            blocks,
            "head",
            0,
            0,
            tiled=True,
            axis_index_groups=line_groups(),
        )
        return jnp.sum(blocks.astype(f32), axis=0)

    def line_gather(block):
        blocks = lax.all_to_all(
            jnp.broadcast_to(block[None], (line, *block.shape)),
            "head",
            0,
            0,
            tiled=True,
            axis_index_groups=line_groups(),
        )
        return blocks.reshape(line * block.shape[0], *block.shape[1:])

    context_pair = jnp.concatenate([context, across(context)])
    out_half = jnp.concatenate(own_half(out_weight))
    attention = line_exchange(
        contract_lead(out_half, context_pair).astype(bf16).reshape(line, rows, frames)
    )
    hidden = (stream.astype(f32) + attention).astype(bf16)

    glu_half = jnp.concatenate(own_half(glu_weight.reshape(2 * rows, width)))
    glu_turned, proj_turned = lax.optimization_barrier(
        (
            glu_half.T,
            jnp.transpose(proj_weight.reshape(rows, 2, line, rows), (2, 1, 3, 0)).reshape(
                width, rows
            ),
        )
    )

    grad_other = across(out_grad)
    hidden, grad_other = lax.optimization_barrier((hidden, grad_other))
    hidden_full = gather(hidden, "head").reshape(width, frames)
    grad_pair = jnp.stack(
        [jnp.where(side == 0, out_grad, grad_other), jnp.where(side == 0, grad_other, out_grad)]
    )
    grad_lines = lax.all_gather(
        grad_pair, "head", axis=1, tiled=False, axis_index_groups=line_groups()
    )
    wide = hidden_full.astype(f32)
    centered = wide - jnp.mean(wide, axis=0, keepdims=True)
    frame_rstd = lax.rsqrt(jnp.mean(centered * centered, axis=0, keepdims=True) + epsilon)
    standard = centered * frame_rstd
    normed = (standard * gain_col + bias_col).astype(bf16)

    pair_out = jnp.einsum("jcd,dt->jct", glu_weight, normed, preferred_element_type=f32)
    glu_value, glu_gate = pair_out[0], pair_out[1]
    gate_sig = jax.nn.sigmoid(glu_gate)
    gated_out = (glu_value * gate_sig).astype(bf16)
    widened = neighbours(gated_out, 2 * half, lanes).astype(f32)
    frames_wide = frames + 2 * half
    conv_wide = depth_kernel[:, 0:1] * widened[:, 0:frames_wide]
    for tap in range(1, taps):
        conv_wide = (
            conv_wide + depth_kernel[:, tap : tap + 1] * widened[:, tap : tap + frames_wide]
        )

    place = lax.axis_index("seq") * frames - half + jnp.arange(lanes)
    inside = (place >= 0) & (place < frames_all) & (jnp.arange(lanes) < frames_wide)
    inside = inside.astype(f32)[None, :]
    conv_wide = jnp.pad(conv_wide, ((0, 0), (0, lanes - frames_wide)))
    conv_out = conv_wide[:, half : half + frames]
    block_mean = jnp.mean(conv_out, axis=1)
    block_cent = conv_out - block_mean[:, None]
    block_square = jnp.sum(block_cent * block_cent, axis=1)
    block, grad_lines = lax.optimization_barrier(
        (jnp.stack([block_mean, block_square]), grad_lines)
    )
    moments = gather(block, "seq")
    grad_full = grad_lines.reshape(width, frames)
    swish_grad = jnp.dot(proj_weight, grad_full, preferred_element_type=f32)
    swish_wide = neighbours(swish_grad, half, lanes)
    chan_mean = jnp.mean(moments[:, 0], axis=0)
    mean_gap = moments[:, 0] - chan_mean
    chan_var = (
        jnp.sum(moments[:, 1], axis=0) + frames * jnp.sum(mean_gap * mean_gap, axis=0)
    ) / frames_all
    chan_rstd = lax.rsqrt(chan_var + epsilon)
    chan_unit = (conv_out - chan_mean[:, None]) * chan_rstd[:, None]
    shifted = chan_unit * bn_gain[:, None] + bn_bias[:, None]
    shift_sig = jax.nn.sigmoid(shifted)
    swished = (shifted * shift_sig).astype(bf16)
    shift_grad = swish_grad * shift_sig * (1.0 + shifted * (1.0 - shift_sig))

    sums = gather(
        jnp.stack([jnp.sum(shift_grad, axis=1), jnp.sum(shift_grad * chan_unit, axis=1)]), "seq"
    )
    bias_total, gain_total = jnp.sum(sums[:, 0], axis=0), jnp.sum(sums[:, 1], axis=0)
    consts = jnp.stack(
        [
            chan_mean,
            chan_rstd,
            bn_gain,
            bn_bias,
            bias_total / frames_all,
            gain_total / frames_all,
        ],
        axis=1,
    )
    pair_grad, grad_wide = conv_back(
        consts, depth_kernel, inside, swish_wide, conv_wide, pair_out, taps
    )

    branch_part = jnp.dot(proj_turned, swished, preferred_element_type=f32).astype(bf16)
    branch_sum = lax.psum_scatter(
        branch_part, "head", scatter_dimension=0, tiled=True, axis_index_groups=line_groups()
    ).reshape(2, rows, frames)
    pair_rows = pair_grad.reshape(2 * rows, frames)
    pair_both = jnp.concatenate([pair_rows, across(pair_rows)])
    normed_part = jnp.dot(glu_turned, pair_both, preferred_element_type=f32).astype(bf16)
    bias_out = jnp.einsum("jcd,d->jc", glu_weight.astype(f32), ln_bias)
    gain_out = jnp.einsum("jcd,d->jc", glu_weight.astype(f32), ln_gain)
    pair_float = pair_grad.astype(f32)
    frame_sums = jnp.stack(
        [
            jnp.sum(pair_float * gain_out[:, :, None], axis=(0, 1)),
            jnp.sum(pair_float * (pair_out - bias_out[:, :, None]), axis=(0, 1)),
        ]
    )
    frame_sums = jnp.pad(frame_sums.astype(bf16), ((0, 14), (0, 0)))
    normed_rows = line_exchange(
        jnp.concatenate(
            [
                normed_part.reshape(line, rows, frames),
                jnp.broadcast_to(frame_sums[None], (line, 16, frames)),
            ],
            axis=1,
        )
    )

    proj_part = contract_last(swished, grad_full)
    glu_part = jnp.einsum("jct,dt->jcd", pair_grad, normed, preferred_element_type=f32)
    early = jnp.concatenate([proj_part[None], glu_part]).reshape(3 * rows, width)
    for bit in (1, parts // 2):
        keep, send = halves(early, bit)
        early = keep + swap_bit(send.astype(bf16), bit).astype(f32)
    normed_rows, early, branch_sum = lax.optimization_barrier((normed_rows, early, branch_sum))

    branch_keep = lax.dynamic_index_in_dim(branch_sum, side, 0, keepdims=False)
    branch_send = lax.dynamic_index_in_dim(branch_sum, 1 - side, 0, keepdims=False)
    branch = branch_keep.astype(f32) + across(branch_send).astype(f32)
    columns = [
        [x * (parts // 2) + 2 * y + core for y in range(parts // 4)]
        for x in range(2)
        for core in range(2)
    ]
    early = lax.all_gather(early.astype(bf16), "seq", axis=0, axis_index_groups=columns)
    kernel_part = taps_grad(grad_wide, widened, taps, frames)[:, :taps]

    def side_half(array):
        return lax.dynamic_slice_in_dim(array, side * (width // 2), width // 2)

    line_sums = normed_rows[rows : rows + 2]
    frame_means = (line_sums + across(line_sums)) / width
    normed_grad = line_gather(normed_rows[:rows].astype(bf16)).astype(f32)
    scaled = normed_grad * side_half(gain_col)
    stream_half = (
        side_half(grad_full).astype(f32)
        + frame_rstd
        * (scaled - frame_means[0:1] - side_half(standard) * frame_means[1:2])
    ).astype(bf16)
    stream_grad = lax.dynamic_slice_in_dim(stream_half, (me % line) * rows, rows)
    context_pair_grad = jnp.dot(out_half, stream_half, preferred_element_type=f32)
    context_grad = (
        context_pair_grad[:rows] + across(context_pair_grad[rows:].astype(bf16)).astype(f32)
    ).astype(bf16)

    out_part = contract_last(context_pair, stream_half)
    out_sides = jnp.concatenate(
        [
            jnp.where(side == 0, out_part[:rows], out_part[rows:]),
            jnp.where(side == 0, out_part[rows:], out_part[:rows]),
        ]
    ).reshape(parts, 2 * rows // parts, width // 2)
    tap_lanes = jnp.pad(kernel_part, ((0, 0), (0, 32 - taps)))
    tap_lanes = tap_lanes.reshape(parts, 2 * rows // parts, 16)
    late = jnp.pad(
        jnp.concatenate([out_sides, tap_lanes], axis=2), ((0, 0), (0, 0), (0, 112))
    ).astype(bf16)
    late, early, branch = lax.optimization_barrier((late, early, branch))
    output = (hidden.astype(f32) + branch).astype(bf16)
    early = jnp.sum(early.astype(f32), axis=0).astype(bf16)
    for bit in (parts // 2, 1):
        early = joined(early, swap_bit(early, bit), bit)
    early = early.astype(f32).reshape(3, rows, width)
    piece = jnp.sum(exchange(late, "seq").astype(f32), axis=0).astype(bf16)
    stays = (lax.axis_index("seq") // (parts // 2)) == side
    moves = [
        (h * parts + s, (h + line) % heads * parts + (s + parts // 2) % parts)
        for h in range(heads)
        for s in range(parts)
        if s // (parts // 2) != h // line
    ]
    moved = lax.ppermute(piece, ("head", "seq"), moves)
    out_lanes = lax.broadcasted_iota(jnp.int32, piece.shape, 1) < width // 2
    piece = jnp.where(out_lanes & ~stays, moved, piece)
    late = gather(piece, "seq")
    out_weight_grad = (
        jnp.swapaxes(late[:, :, : width // 2].reshape(2, rows, width // 2), 0, 1)
        .reshape(rows, width)
        .astype(f32)
    )
    kernel_grad = late[:, :, width // 2 : width // 2 + 16].reshape(rows, 32)[:, :taps].astype(f32)
    return (
        output,
        stream_grad,
        context_grad,
        out_weight_grad,
        early[1:],
        kernel_grad,
        gain_total,
        bias_total,
        early[0],
    )


def solution(mesh):
    return jax.shard_map(
        on_device,
        mesh=mesh,
        in_specs=(
            P("head", "seq"),
            P("head", "seq"),
            P("head", None),
            P(),
            P(),
            P(None, "head", None),
            P("head", None),
            P("head"),
            P("head"),
            P("head", None),
            P("head", "seq"),
        ),
        out_specs=(
            P("head", "seq"),
            P("head", "seq"),
            P("head", "seq"),
            P("head", None),
            P(None, "head", None),
            P("head", None),
            P("head"),
            P("head"),
            P("head", None),
        ),
        check_vma=False,
    )
```

```python
import functools

import jax
import jax.numpy as jnp
from jax import lax
from jax.experimental import pallas as pl
from jax.experimental.pallas import tpu as pltpu
from jax.sharding import PartitionSpec as P

epsilon = 1e-05
f32 = jnp.float32
bf16 = jnp.bfloat16


def contract_lead(first_op, second_op):
    return lax.dot_general(
        first_op, second_op, (((0,), (0,)), ((), ())), preferred_element_type=f32
    )


def contract_last(first_op, second_op):
    return lax.dot_general(
        first_op, second_op, (((1,), (1,)), ((), ())), preferred_element_type=f32
    )


def exchange(blocks, axis):
    return lax.all_to_all(blocks, axis, 0, 0, tiled=True)


def gather(block, axis):
    count = lax.axis_size(axis)
    copies = jnp.broadcast_to(block[None], (count, *block.shape))
    return exchange(copies, axis)


def line_groups():
    half = lax.axis_size("head") // 2
    return [[side * half + i for i in range(half)] for side in range(2)]


def across(operand):
    count = lax.axis_size("head")
    return lax.ppermute(operand, "head", [(i, (i + count // 2) % count) for i in range(count)])


def swap_bit(operand, bit):
    count = lax.axis_size("seq")
    return lax.ppermute(operand, "seq", [(i, i ^ bit) for i in range(count)])


def halves(operand, bit):
    mine = (lax.axis_index("seq") // bit) % 2
    size = operand.shape[0] // 2
    keep = lax.dynamic_slice_in_dim(operand, mine * size, size)
    send = lax.dynamic_slice_in_dim(operand, (1 - mine) * size, size)
    return keep, send


def joined(mine_rows, other_rows, bit):
    low = (lax.axis_index("seq") // bit) % 2 == 0
    return jnp.concatenate(
        [jnp.where(low, mine_rows, other_rows), jnp.where(low, other_rows, mine_rows)]
    )


def shifted_left(operand, distance):
    lanes = operand.shape[1]
    return pltpu.roll(operand, (lanes - distance) % lanes, 1)


def conv_back_kernel(
    consts_ref, taps_ref, inside_ref, swish_ref, conv_ref, pair_out_ref, pair_ref, grad_ref, *, taps
):
    frames = pair_ref.shape[2]

    def chunk(index, carry):
        at = pl.ds(pl.multiple_of(index * 16, 16), 16)
        consts = consts_ref[at, :]
        mean, rstd, gain, bias = (consts[:, i : i + 1] for i in range(4))
        bias_mean, gain_mean = consts[:, 4:5], consts[:, 5:6]
        unit = (conv_ref[at, :] - mean) * rstd
        shifted = unit * gain + bias
        sig = jax.nn.sigmoid(shifted)
        shift_grad = swish_ref[at, :] * sig * (1.0 + shifted * (1.0 - sig))
        grad = rstd * gain * (shift_grad - bias_mean - unit * gain_mean)
        grad = jnp.where(inside_ref[...] > 0.0, grad, 0.0).astype(bf16).astype(f32)
        grad_ref[at, :] = grad
        kernel = taps_ref[at, :]
        total = kernel[:, 0:1] * shifted_left(grad, taps - 1)[:, :frames]
        for tap in range(1, taps):
            total = total + kernel[:, tap : tap + 1] * shifted_left(grad, taps - 1 - tap)[:, :frames]
        gate_sig = jax.nn.sigmoid(pair_out_ref[1, at, :])
        value_grad = total * gate_sig
        pair_ref[0, at, :] = value_grad.astype(bf16)
        pair_ref[1, at, :] = (value_grad * pair_out_ref[0, at, :] * (1.0 - gate_sig)).astype(bf16)
        return carry

    lax.fori_loop(0, pair_ref.shape[1] // 16, chunk, 0)


def line_product_kernel(weight_ref, operand_ref, extra_ref, out_ref):
    lines, held, _ = out_ref.shape
    rows = weight_ref.shape[0] // lines
    product = jnp.dot(weight_ref[...], operand_ref[...], preferred_element_type=f32).astype(bf16)
    for index in range(lines):
        out_ref[index, :rows, :] = product[index * rows : (index + 1) * rows]
        out_ref[index, rows:held, :] = extra_ref[...]


def line_product(weight, operand, extra, lines):
    held = weight.shape[0] // lines + extra.shape[0]
    return pl.pallas_call(
        line_product_kernel,
        out_shape=jax.ShapeDtypeStruct((lines, held, operand.shape[1]), bf16),
        compiler_params=pltpu.CompilerParams(vmem_limit_bytes=32 * 1024 * 1024),
        name="line_product",
    )(weight, operand, extra)


def taps_grad_kernel(grad_ref, widened_ref, out_ref, lane_sums, *, taps, frames):
    half = taps // 2
    rows, lanes = grad_ref.shape
    inside = lax.broadcasted_iota(jnp.int32, (16, lanes), 1) < frames

    def chunk(index, carry):
        first = pl.multiple_of(index * 16, 16)
        grad = jnp.where(inside, shifted_left(grad_ref[pl.ds(first, 16), :], half), 0.0)
        widened = widened_ref[pl.ds(first, 16), :].astype(f32)
        for tap in range(taps):
            product = grad * shifted_left(widened, half + tap)
            total = product[:, :128]
            for lane in range(128, lanes, 128):
                total = total + product[:, lane : lane + 128]
            lane_sums[pl.ds(pl.multiple_of(tap * rows + first, 16), 16), :] = total
        return carry

    lax.fori_loop(0, rows // 16, chunk, 0)
    out_ref[...] = lax.dot_general(
        jnp.ones((8, 128), f32),
        lane_sums[...],
        (((1,), (1,)), ((), ())),
        preferred_element_type=f32,
        precision=lax.Precision.HIGHEST,
    )


def conv_back(consts, kernel, inside, swish_wide, conv_wide, pair_out, taps):
    return pl.pallas_call(
        functools.partial(conv_back_kernel, taps=taps),
        out_shape=(
            jax.ShapeDtypeStruct(pair_out.shape, bf16),
            jax.ShapeDtypeStruct(conv_wide.shape, f32),
        ),
        name="conv_back",
    )(consts, kernel, inside, swish_wide, conv_wide, pair_out)


def taps_grad(grad_wide, widened, taps, frames):
    rows = grad_wide.shape[0]
    sums = pl.pallas_call(
        functools.partial(taps_grad_kernel, taps=taps, frames=frames),
        out_shape=jax.ShapeDtypeStruct((8, taps * rows), f32),
        scratch_shapes=[pltpu.VMEM((taps * rows, 128), f32)],
        name="taps_grad",
    )(grad_wide, widened)
    return sums[0].reshape(taps, rows).T


def neighbours(operand, half_width):
    count, length = lax.axis_size("seq"), operand.shape[1]
    up = [(i, (i + 1) % count) for i in range(count - 1)]
    down = [(j, i) for i, j in up]
    before = lax.ppermute(operand[:, length - half_width :], "seq", up)
    after = lax.ppermute(operand[:, :half_width], "seq", down)
    return jnp.concatenate([before, operand, after], axis=1)


def on_device(
    context,
    stream,
    out_weight,
    ln_gain,
    ln_bias,
    glu_weight,
    depth_kernel,
    bn_gain,
    bn_bias,
    proj_weight,
    out_grad,
):
    rows, frames = stream.shape
    width = ln_gain.shape[0]
    heads = lax.axis_size("head")
    parts = lax.axis_size("seq")
    frames_all = frames * parts
    taps = depth_kernel.shape[1]
    half = taps // 2
    lanes = -(-(frames + 4 * half) // 128) * 128
    me = lax.axis_index("head")
    line = heads // 2
    side = me // line
    gain_col = ln_gain[:, None]
    bias_col = ln_bias[:, None]

    def own_half(weight):
        keep = lax.dynamic_slice_in_dim(weight, side * (width // 2), width // 2, axis=1)
        send = lax.dynamic_slice_in_dim(weight, (1 - side) * (width // 2), width // 2, axis=1)
        return keep, across(send)

    def line_exchange(blocks):
        blocks = lax.all_to_all(
            blocks,
            "head",
            0,
            0,
            tiled=True,
            axis_index_groups=line_groups(),
        )
        return jnp.sum(blocks.astype(f32), axis=0)

    def line_gather(block):
        blocks = lax.all_to_all(
            jnp.broadcast_to(block[None], (line, *block.shape)),
            "head",
            0,
            0,
            tiled=True,
            axis_index_groups=line_groups(),
        )
        return blocks.reshape(line * block.shape[0], *block.shape[1:])

    out_keep = lax.dynamic_slice_in_dim(out_weight, side * (width // 2), width // 2, axis=1)
    out_send = lax.dynamic_slice_in_dim(out_weight, (1 - side) * (width // 2), width // 2, axis=1)
    swapped = across(jnp.concatenate([context, out_send], axis=1))
    context_pair = jnp.concatenate([context, swapped[:, :frames]])
    out_half = jnp.concatenate([out_keep, swapped[:, frames:]])
    attention = line_exchange(
        contract_lead(out_half, context_pair).astype(bf16).reshape(line, rows, frames)
    )
    hidden = (stream.astype(f32) + attention).astype(bf16)

    glu_half = jnp.concatenate(own_half(glu_weight.reshape(2 * rows, width)))
    proj_half = jnp.concatenate(own_half(proj_weight))
    glu_turned, proj_turned = lax.optimization_barrier((glu_half.T, proj_half.T))

    frames_wide = frames + 2 * half
    grad_mine = neighbours(out_grad, half)
    grad_other = across(grad_mine)
    grad_pair = jnp.stack(
        [jnp.where(side == 0, grad_mine, grad_other), jnp.where(side == 0, grad_other, grad_mine)]
    )
    hidden, _ = lax.optimization_barrier((hidden, grad_pair))
    grad_lines = lax.all_gather(
        grad_pair, "head", axis=1, tiled=False, axis_index_groups=line_groups()
    )

    def side_half(array):
        return lax.dynamic_slice_in_dim(array, side * (width // 2), width // 2)

    def in_order(mine, other, axis):
        return jnp.concatenate(
            [jnp.where(side == 0, mine, other), jnp.where(side == 0, other, mine)], axis=axis
        )

    glu_own = glu_weight.astype(f32)
    gain_outs = jnp.einsum("jcsd,sd->sjc", glu_own.reshape(2, rows, 2, -1), ln_gain.reshape(2, -1))
    gain_gap = jnp.where(side == 0, gain_outs[0] - gain_outs[1], gain_outs[1] - gain_outs[0])
    gain_out = gain_outs[0] + gain_outs[1]
    bias_out = jnp.einsum("jcd,d->jc", glu_own, ln_bias)

    hidden_half = line_gather(hidden)
    half_float = hidden_half.astype(f32)
    half_mean = jnp.mean(half_float, axis=0, keepdims=True)
    half_cent = half_float - half_mean
    half_square = jnp.sum(half_cent * half_cent, axis=0, keepdims=True)
    half_moments = jnp.concatenate([half_mean, half_square])
    other_moments = across(half_moments)
    gained = (half_cent * side_half(gain_col)).astype(bf16)
    products = jnp.dot(glu_half, gained, preferred_element_type=f32)
    other_products = across(products[2 * rows :].astype(bf16)).astype(f32)
    mean_gap = 0.5 * (half_moments[0:1] - other_moments[0:1])
    frame_mean = half_moments[0:1] - mean_gap
    frame_var = (
        half_moments[1:2] + other_moments[1:2] + width * mean_gap * mean_gap
    ) / width
    frame_rstd = lax.rsqrt(frame_var + epsilon)
    products = (products[: 2 * rows] + other_products).reshape(2, rows, frames)
    pair_out = (
        frame_rstd * (products + mean_gap * gain_gap[:, :, None]) + bias_out[:, :, None]
    )
    glu_value, glu_gate = pair_out[0], pair_out[1]
    gate_sig = jax.nn.sigmoid(glu_gate)
    gated_out = (glu_value * gate_sig).astype(bf16)
    widened = neighbours(gated_out, 2 * half)
    widened = jnp.pad(widened, ((0, 0), (0, lanes - widened.shape[1])))
    widened = widened.astype(f32)
    conv_wide = depth_kernel[:, 0:1] * widened[:, 0:frames_wide]
    for tap in range(1, taps):
        conv_wide = (
            conv_wide + depth_kernel[:, tap : tap + 1] * widened[:, tap : tap + frames_wide]
        )

    place = lax.axis_index("seq") * frames - half + jnp.arange(lanes)
    inside = (place >= 0) & (place < frames_all) & (jnp.arange(lanes) < frames_wide)
    inside = inside.astype(f32)[None, :]
    conv_wide = jnp.pad(conv_wide, ((0, 0), (0, lanes - frames_wide)))
    conv_out = conv_wide[:, half : half + frames]
    block_mean = jnp.mean(conv_out, axis=1)
    block_cent = conv_out - block_mean[:, None]
    block_square = jnp.sum(block_cent * block_cent, axis=1)
    moments = gather(jnp.stack([block_mean, block_square]), "seq")
    moments, grad_lines = lax.optimization_barrier((moments, grad_lines))
    grad_full = grad_lines.reshape(width, frames_wide)
    swish_wide = jnp.dot(proj_weight, grad_full, preferred_element_type=f32)
    swish_grad = swish_wide[:, half : half + frames]
    swish_wide = jnp.pad(swish_wide, ((0, 0), (0, lanes - frames_wide)))
    grad_half = lax.dynamic_index_in_dim(grad_lines, side, 0, keepdims=False)
    grad_half = grad_half.reshape(width // 2, frames_wide)[:, half : half + frames]
    chan_mean = jnp.mean(moments[:, 0], axis=0)
    mean_gap = moments[:, 0] - chan_mean
    chan_var = (
        jnp.sum(moments[:, 1], axis=0) + frames * jnp.sum(mean_gap * mean_gap, axis=0)
    ) / frames_all
    chan_rstd = lax.rsqrt(chan_var + epsilon)
    chan_unit = (conv_out - chan_mean[:, None]) * chan_rstd[:, None]
    shifted = chan_unit * bn_gain[:, None] + bn_bias[:, None]
    shift_sig = jax.nn.sigmoid(shifted)
    swished = (shifted * shift_sig).astype(bf16)
    shift_grad = swish_grad * shift_sig * (1.0 + shifted * (1.0 - shift_sig))

    sums = gather(
        jnp.stack([jnp.sum(shift_grad, axis=1), jnp.sum(shift_grad * chan_unit, axis=1)]), "seq"
    )
    bias_total, gain_total = jnp.sum(sums[:, 0], axis=0), jnp.sum(sums[:, 1], axis=0)
    consts = jnp.stack(
        [
            chan_mean,
            chan_rstd,
            bn_gain,
            bn_bias,
            bias_total / frames_all,
            gain_total / frames_all,
        ],
        axis=1,
    )
    pair_grad, grad_wide = conv_back(
        consts, depth_kernel, inside, swish_wide, conv_wide, pair_out, taps
    )

    pair_rows = pair_grad.reshape(2 * rows, frames)
    other_rows = across(jnp.concatenate([pair_rows, swished]))
    pair_both = jnp.concatenate([pair_rows, other_rows[: 2 * rows]])
    swished_pair = jnp.concatenate([swished, other_rows[2 * rows :]])
    pair_float = pair_grad.astype(f32)
    frame_sums = jnp.stack(
        [
            jnp.sum(pair_float * gain_out[:, :, None], axis=(0, 1)),
            jnp.sum(pair_float * (pair_out - bias_out[:, :, None]), axis=(0, 1)),
        ]
    )
    frame_sums = jnp.pad(frame_sums.astype(bf16), ((0, 14), (0, 0)))
    normed_rows = line_exchange(line_product(glu_turned, pair_both, frame_sums, line))

    standard = (half_float - frame_mean) * frame_rstd
    normed_half = (standard * side_half(gain_col) + side_half(bias_col)).astype(bf16)
    proj_part = contract_last(jnp.pad(swished, ((0, 0), (half, half))), grad_full)
    glu_part = contract_last(pair_both, normed_half)
    glu_part = jnp.concatenate([glu_part[: 2 * rows], glu_part[2 * rows :]], axis=1)
    early = jnp.concatenate([proj_part, glu_part])
    kernel_part = taps_grad(grad_wide, widened, taps, frames)
    for bit in (1, parts // 2):
        keep, send = halves(early, bit)
        early = keep + swap_bit(send.astype(bf16), bit).astype(f32)
    normed_rows, early = lax.optimization_barrier((normed_rows, early))
    columns = [
        [x * (parts // 2) + 2 * y + core for y in range(parts // 4)]
        for x in range(2)
        for core in range(2)
    ]
    early = lax.all_gather(early.astype(bf16), "seq", axis=0, axis_index_groups=columns)

    line_sums = normed_rows[rows : rows + 2]
    frame_means = (line_sums + across(line_sums)) / width
    normed_grad = line_gather(normed_rows[:rows].astype(bf16))

    branch_part = line_product(
        proj_turned, swished_pair, jnp.zeros((rows, frames), bf16), line
    ).reshape(2 * line * rows, frames)
    normed_grad, branch_part = lax.optimization_barrier((normed_grad, branch_part))
    branch = lax.psum_scatter(
        branch_part, "head", scatter_dimension=0, tiled=True, axis_index_groups=line_groups()
    )[:rows]
    output = (hidden.astype(f32) + branch.astype(f32)).astype(bf16)

    normed_grad = normed_grad.astype(f32)
    scaled = normed_grad * side_half(gain_col)
    stream_half = (
        grad_half.astype(f32)
        + frame_rstd
        * (scaled - frame_means[0:1] - standard * frame_means[1:2])
    ).astype(bf16)
    stream_grad = lax.dynamic_slice_in_dim(stream_half, (me % line) * rows, rows)
    context_pair_grad = jnp.dot(out_half, stream_half, preferred_element_type=f32)

    out_part = contract_last(context_pair, stream_half)
    out_sides = jnp.concatenate(
        [
            jnp.where(side == 0, out_part[:rows], out_part[rows:]),
            jnp.where(side == 0, out_part[rows:], out_part[:rows]),
        ]
    ).reshape(parts, 2 * rows // parts, width // 2)
    tap_lanes = jnp.pad(kernel_part, ((0, 0), (0, 32 - taps)))
    tap_lanes = tap_lanes.reshape(parts, 2 * rows // parts, 16)
    late = jnp.pad(
        jnp.concatenate([out_sides, tap_lanes], axis=2), ((0, 0), (0, 0), (0, 112))
    ).astype(bf16)
    early = jnp.sum(early.astype(f32), axis=0).astype(bf16)
    early_other = across(early[:, width // 2 :])
    seq = lax.axis_index("seq")
    first_row = (seq % 2) * (2 * early.shape[0]) + (seq // (parts // 2)) * early.shape[0]
    is_glu = (first_row + jnp.arange(early.shape[0]) >= rows)[:, None]
    early = jnp.where(is_glu, in_order(early[:, : width // 2], early_other, 1), early)
    piece = jnp.sum(exchange(late, "seq").astype(f32), axis=0).astype(bf16)
    context_send = context_pair_grad[rows:].astype(bf16)
    piece, early = lax.optimization_barrier((piece, early))
    early = joined(early, swap_bit(early, parts // 2), parts // 2)
    context_send, early = lax.optimization_barrier((context_send, early))
    context_grad = (context_pair_grad[:rows] + across(context_send).astype(f32)).astype(bf16)
    early = joined(early, swap_bit(early, 1), 1)
    early = early.astype(f32).reshape(3, rows, width)
    stays = (lax.axis_index("seq") // (parts // 2)) == side
    moves = [
        (h * parts + s, (h + line) % heads * parts + (s + parts // 2) % parts)
        for h in range(heads)
        for s in range(parts)
        if s // (parts // 2) != h // line
    ]
    moved = lax.ppermute(piece, ("head", "seq"), moves)
    out_lanes = lax.broadcasted_iota(jnp.int32, piece.shape, 1) < width // 2
    piece = jnp.where(out_lanes & ~stays, moved, piece)
    late = gather(piece, "seq")
    out_weight_grad = (
        jnp.swapaxes(late[:, :, : width // 2].reshape(2, rows, width // 2), 0, 1)
        .reshape(rows, width)
        .astype(f32)
    )
    kernel_grad = late[:, :, width // 2 : width // 2 + 16].reshape(rows, 32)[:, :taps].astype(f32)
    return (
        output,
        stream_grad,
        context_grad,
        out_weight_grad,
        early[1:],
        kernel_grad,
        gain_total,
        bias_total,
        early[0],
    )


def solution(mesh):
    return jax.shard_map(
        on_device,
        mesh=mesh,
        in_specs=(
            P("head", "seq"),
            P("head", "seq"),
            P("head", None),
            P(),
            P(),
            P(None, "head", None),
            P("head", None),
            P("head"),
            P("head"),
            P("head", None),
            P("head", "seq"),
        ),
        out_specs=(
            P("head", "seq"),
            P("head", "seq"),
            P("head", "seq"),
            P("head", None),
            P(None, "head", None),
            P("head", None),
            P("head"),
            P("head"),
            P("head", None),
        ),
        check_vma=False,
    )
```

```python
import functools

import jax
import jax.numpy as jnp
from jax import lax
from jax.experimental import pallas as pl
from jax.experimental.pallas import tpu as pltpu
from jax.sharding import PartitionSpec as P

epsilon = 1e-05
f32 = jnp.float32
bf16 = jnp.bfloat16


def contract_lead(first_op, second_op):
    return lax.dot_general(
        first_op, second_op, (((0,), (0,)), ((), ())), preferred_element_type=f32
    )


def contract_last(first_op, second_op):
    return lax.dot_general(
        first_op, second_op, (((1,), (1,)), ((), ())), preferred_element_type=f32
    )


def exchange(blocks, axis):
    return lax.all_to_all(blocks, axis, 0, 0, tiled=True)


def gather(block, axis):
    count = lax.axis_size(axis)
    copies = jnp.broadcast_to(block[None], (count, *block.shape))
    return exchange(copies, axis)


def line_groups():
    half = lax.axis_size("head") // 2
    return [[side * half + i for i in range(half)] for side in range(2)]


def across(operand):
    count = lax.axis_size("head")
    return lax.ppermute(operand, "head", [(i, (i + count // 2) % count) for i in range(count)])


def swap_bit(operand, bit):
    count = lax.axis_size("seq")
    return lax.ppermute(operand, "seq", [(i, i ^ bit) for i in range(count)])


def halves(operand, bit):
    mine = (lax.axis_index("seq") // bit) % 2
    size = operand.shape[0] // 2
    keep = lax.dynamic_slice_in_dim(operand, mine * size, size)
    send = lax.dynamic_slice_in_dim(operand, (1 - mine) * size, size)
    return keep, send


def joined(mine_rows, other_rows, bit):
    low = (lax.axis_index("seq") // bit) % 2 == 0
    return jnp.concatenate(
        [jnp.where(low, mine_rows, other_rows), jnp.where(low, other_rows, mine_rows)]
    )


def shifted_left(operand, distance):
    lanes = operand.shape[1]
    return pltpu.roll(operand, (lanes - distance) % lanes, 1)


def conv_back_kernel(
    consts_ref, taps_ref, inside_ref, swish_ref, conv_ref, pair_out_ref, pair_ref, grad_ref, *, taps
):
    frames = pair_ref.shape[2]

    def chunk(index, carry):
        at = pl.ds(pl.multiple_of(index * 16, 16), 16)
        consts = consts_ref[at, :]
        mean, rstd, gain, bias = (consts[:, i : i + 1] for i in range(4))
        bias_mean, gain_mean = consts[:, 4:5], consts[:, 5:6]
        unit = (conv_ref[at, :] - mean) * rstd
        shifted = unit * gain + bias
        sig = jax.nn.sigmoid(shifted)
        shift_grad = swish_ref[at, :] * sig * (1.0 + shifted * (1.0 - sig))
        grad = rstd * gain * (shift_grad - bias_mean - unit * gain_mean)
        grad = jnp.where(inside_ref[...] > 0.0, grad, 0.0).astype(bf16).astype(f32)
        grad_ref[at, :] = grad
        kernel = taps_ref[at, :]
        total = kernel[:, 0:1] * shifted_left(grad, taps - 1)[:, :frames]
        for tap in range(1, taps):
            total = total + kernel[:, tap : tap + 1] * shifted_left(grad, taps - 1 - tap)[:, :frames]
        gate_sig = jax.nn.sigmoid(pair_out_ref[1, at, :])
        value_grad = total * gate_sig
        pair_ref[0, at, :] = value_grad.astype(bf16)
        pair_ref[1, at, :] = (value_grad * pair_out_ref[0, at, :] * (1.0 - gate_sig)).astype(bf16)
        return carry

    lax.fori_loop(0, pair_ref.shape[1] // 16, chunk, 0)


def line_product_kernel(weight_ref, operand_ref, extra_ref, out_ref):
    lines, rows, lanes = out_ref.shape
    frames = operand_ref.shape[1]
    product = jnp.dot(weight_ref[...], operand_ref[...], preferred_element_type=f32).astype(bf16)
    for index in range(lines):
        out_ref[index, :, :frames] = product[index * rows : (index + 1) * rows]
        out_ref[index, :, frames:lanes] = extra_ref[...]


def line_product(weight, operand, extra, lines):
    rows, lanes = extra.shape[0], operand.shape[1] + extra.shape[1]
    return pl.pallas_call(
        line_product_kernel,
        out_shape=jax.ShapeDtypeStruct((lines, rows, lanes), bf16),
        compiler_params=pltpu.CompilerParams(vmem_limit_bytes=32 * 1024 * 1024),
        name="line_product",
    )(weight, operand, extra)


def taps_grad_kernel(grad_ref, widened_ref, out_ref, lane_sums, *, taps, frames):
    half = taps // 2
    rows, lanes = grad_ref.shape
    inside = lax.broadcasted_iota(jnp.int32, (16, lanes), 1) < frames

    def chunk(index, carry):
        first = pl.multiple_of(index * 16, 16)
        grad = jnp.where(inside, shifted_left(grad_ref[pl.ds(first, 16), :], half), 0.0)
        widened = widened_ref[pl.ds(first, 16), :].astype(f32)
        for tap in range(taps):
            product = grad * shifted_left(widened, half + tap)
            total = product[:, :128]
            for lane in range(128, lanes, 128):
                total = total + product[:, lane : lane + 128]
            lane_sums[pl.ds(pl.multiple_of(tap * rows + first, 16), 16), :] = total
        return carry

    lax.fori_loop(0, rows // 16, chunk, 0)
    out_ref[...] = lax.dot_general(
        jnp.ones((8, 128), f32),
        lane_sums[...],
        (((1,), (1,)), ((), ())),
        preferred_element_type=f32,
        precision=lax.Precision.HIGHEST,
    )


def conv_back(consts, kernel, inside, swish_wide, conv_wide, pair_out, taps):
    return pl.pallas_call(
        functools.partial(conv_back_kernel, taps=taps),
        out_shape=(
            jax.ShapeDtypeStruct(pair_out.shape, bf16),
            jax.ShapeDtypeStruct(conv_wide.shape, f32),
        ),
        name="conv_back",
    )(consts, kernel, inside, swish_wide, conv_wide, pair_out)


def taps_grad(grad_wide, widened, taps, frames):
    rows = grad_wide.shape[0]
    sums = pl.pallas_call(
        functools.partial(taps_grad_kernel, taps=taps, frames=frames),
        out_shape=jax.ShapeDtypeStruct((8, taps * rows), f32),
        scratch_shapes=[pltpu.VMEM((taps * rows, 128), f32)],
        name="taps_grad",
    )(grad_wide, widened)
    return sums[0].reshape(taps, rows).T


def neighbours(operand, half_width):
    count, length = lax.axis_size("seq"), operand.shape[1]
    up = [(i, (i + 1) % count) for i in range(count - 1)]
    down = [(j, i) for i, j in up]
    before = lax.ppermute(operand[:, length - half_width :], "seq", up)
    after = lax.ppermute(operand[:, :half_width], "seq", down)
    return jnp.concatenate([before, operand, after], axis=1)


def on_device(
    context,
    stream,
    out_weight,
    ln_gain,
    ln_bias,
    glu_weight,
    depth_kernel,
    bn_gain,
    bn_bias,
    proj_weight,
    out_grad,
):
    rows, frames = stream.shape
    width = ln_gain.shape[0]
    heads = lax.axis_size("head")
    parts = lax.axis_size("seq")
    frames_all = frames * parts
    taps = depth_kernel.shape[1]
    half = taps // 2
    lanes = -(-(frames + 4 * half) // 128) * 128
    me = lax.axis_index("head")
    line = heads // 2
    side = me // line
    gain_col = ln_gain[:, None]
    bias_col = ln_bias[:, None]

    def own_half(weight):
        keep = lax.dynamic_slice_in_dim(weight, side * (width // 2), width // 2, axis=1)
        send = lax.dynamic_slice_in_dim(weight, (1 - side) * (width // 2), width // 2, axis=1)
        return keep, across(send)

    def line_exchange(blocks):
        blocks = lax.all_to_all(
            blocks,
            "head",
            0,
            0,
            tiled=True,
            axis_index_groups=line_groups(),
        )
        return jnp.sum(blocks.astype(f32), axis=0)

    def line_gather(block):
        blocks = lax.all_to_all(
            jnp.broadcast_to(block[None], (line, *block.shape)),
            "head",
            0,
            0,
            tiled=True,
            axis_index_groups=line_groups(),
        )
        return blocks.reshape(line * block.shape[0], *block.shape[1:])

    out_keep = lax.dynamic_slice_in_dim(out_weight, side * (width // 2), width // 2, axis=1)
    out_send = lax.dynamic_slice_in_dim(out_weight, (1 - side) * (width // 2), width // 2, axis=1)
    swapped = across(jnp.concatenate([context, out_send], axis=1))
    context_pair = jnp.concatenate([context, swapped[:, :frames]])
    out_half = jnp.concatenate([out_keep, swapped[:, frames:]])
    attention = line_exchange(
        contract_lead(out_half, context_pair).astype(bf16).reshape(line, rows, frames)
    )
    hidden = (stream.astype(f32) + attention).astype(bf16)

    glu_half = jnp.concatenate(own_half(glu_weight.reshape(2 * rows, width)))
    proj_half = jnp.concatenate(own_half(proj_weight))
    glu_turned, proj_turned = lax.optimization_barrier((glu_half.T, proj_half.T))

    frames_wide = frames + 2 * half
    grad_mine = neighbours(out_grad, half)
    grad_other = across(grad_mine)
    grad_pair = jnp.stack(
        [jnp.where(side == 0, grad_mine, grad_other), jnp.where(side == 0, grad_other, grad_mine)]
    )
    hidden, _ = lax.optimization_barrier((hidden, grad_pair))
    grad_lines = lax.all_gather(
        grad_pair, "head", axis=1, tiled=False, axis_index_groups=line_groups()
    )

    def side_half(array):
        return lax.dynamic_slice_in_dim(array, side * (width // 2), width // 2)

    def in_order(mine, other, axis):
        return jnp.concatenate(
            [jnp.where(side == 0, mine, other), jnp.where(side == 0, other, mine)], axis=axis
        )

    glu_own = glu_weight.astype(f32)
    gain_outs = jnp.einsum("jcsd,sd->sjc", glu_own.reshape(2, rows, 2, -1), ln_gain.reshape(2, -1))
    gain_gap = jnp.where(side == 0, gain_outs[0] - gain_outs[1], gain_outs[1] - gain_outs[0])
    gain_out = gain_outs[0] + gain_outs[1]
    bias_out = jnp.einsum("jcd,d->jc", glu_own, ln_bias)

    hidden_half = line_gather(hidden)
    half_float = hidden_half.astype(f32)
    half_mean = jnp.mean(half_float, axis=0, keepdims=True)
    half_cent = half_float - half_mean
    half_square = jnp.sum(half_cent * half_cent, axis=0, keepdims=True)
    half_moments = jnp.concatenate([half_mean, half_square])
    other_moments = across(half_moments)
    gained = (half_cent * side_half(gain_col)).astype(bf16)
    products = jnp.dot(glu_half, gained, preferred_element_type=f32)
    other_products = across(products[2 * rows :].astype(bf16)).astype(f32)
    mean_gap = 0.5 * (half_moments[0:1] - other_moments[0:1])
    frame_mean = half_moments[0:1] - mean_gap
    frame_var = (
        half_moments[1:2] + other_moments[1:2] + width * mean_gap * mean_gap
    ) / width
    frame_rstd = lax.rsqrt(frame_var + epsilon)
    products = (products[: 2 * rows] + other_products).reshape(2, rows, frames)
    pair_out = (
        frame_rstd * (products + mean_gap * gain_gap[:, :, None]) + bias_out[:, :, None]
    )
    glu_value, glu_gate = pair_out[0], pair_out[1]
    gate_sig = jax.nn.sigmoid(glu_gate)
    gated_out = (glu_value * gate_sig).astype(bf16)
    widened = neighbours(gated_out, 2 * half)
    widened = jnp.pad(widened, ((0, 0), (0, lanes - widened.shape[1])))
    widened = widened.astype(f32)
    conv_wide = depth_kernel[:, 0:1] * widened[:, 0:frames_wide]
    for tap in range(1, taps):
        conv_wide = (
            conv_wide + depth_kernel[:, tap : tap + 1] * widened[:, tap : tap + frames_wide]
        )

    place = lax.axis_index("seq") * frames - half + jnp.arange(lanes)
    inside = (place >= 0) & (place < frames_all) & (jnp.arange(lanes) < frames_wide)
    inside = inside.astype(f32)[None, :]
    conv_wide = jnp.pad(conv_wide, ((0, 0), (0, lanes - frames_wide)))
    conv_out = conv_wide[:, half : half + frames]
    block_mean = jnp.mean(conv_out, axis=1)
    block_cent = conv_out - block_mean[:, None]
    block_square = jnp.sum(block_cent * block_cent, axis=1)
    moments = gather(jnp.stack([block_mean, block_square]), "seq")
    moments, grad_lines = lax.optimization_barrier((moments, grad_lines))
    grad_full = grad_lines.reshape(width, frames_wide)
    swish_wide = jnp.dot(proj_weight, grad_full, preferred_element_type=f32)
    swish_grad = swish_wide[:, half : half + frames]
    swish_wide = jnp.pad(swish_wide, ((0, 0), (0, lanes - frames_wide)))
    grad_half = lax.dynamic_index_in_dim(grad_lines, side, 0, keepdims=False)
    grad_half = grad_half.reshape(width // 2, frames_wide)[:, half : half + frames]
    chan_mean = jnp.mean(moments[:, 0], axis=0)
    mean_gap = moments[:, 0] - chan_mean
    chan_var = (
        jnp.sum(moments[:, 1], axis=0) + frames * jnp.sum(mean_gap * mean_gap, axis=0)
    ) / frames_all
    chan_rstd = lax.rsqrt(chan_var + epsilon)
    chan_unit = (conv_out - chan_mean[:, None]) * chan_rstd[:, None]
    shifted = chan_unit * bn_gain[:, None] + bn_bias[:, None]
    shift_sig = jax.nn.sigmoid(shifted)
    swished = (shifted * shift_sig).astype(bf16)
    shift_grad = swish_grad * shift_sig * (1.0 + shifted * (1.0 - shift_sig))

    sums = gather(
        jnp.stack([jnp.sum(shift_grad, axis=1), jnp.sum(shift_grad * chan_unit, axis=1)]), "seq"
    )
    bias_total, gain_total = jnp.sum(sums[:, 0], axis=0), jnp.sum(sums[:, 1], axis=0)
    consts = jnp.stack(
        [
            chan_mean,
            chan_rstd,
            bn_gain,
            bn_bias,
            bias_total / frames_all,
            gain_total / frames_all,
        ],
        axis=1,
    )
    pair_grad, grad_wide = conv_back(
        consts, depth_kernel, inside, swish_wide, conv_wide, pair_out, taps
    )

    pair_rows = pair_grad.reshape(2 * rows, frames)
    other_rows = across(jnp.concatenate([pair_rows, swished]))
    pair_both = jnp.concatenate([pair_rows, other_rows[: 2 * rows]])
    swished_pair = jnp.concatenate([swished, other_rows[2 * rows :]])
    pair_float = pair_grad.astype(f32)
    frame_sums = jnp.stack(
        [
            jnp.sum(pair_float * gain_out[:, :, None], axis=(0, 1)),
            jnp.sum(pair_float * (pair_out - bias_out[:, :, None]), axis=(0, 1)),
        ]
    )
    spare = lanes - frames
    sum_rows = 2 * frames // spare
    frame_sums = jnp.pad(
        frame_sums.astype(bf16).reshape(sum_rows, spare), ((0, rows - sum_rows), (0, 0))
    )
    normed_rows = line_exchange(line_product(glu_turned, pair_both, frame_sums, line))

    standard = (half_float - frame_mean) * frame_rstd
    normed_half = (standard * side_half(gain_col) + side_half(bias_col)).astype(bf16)
    proj_part = contract_last(jnp.pad(swished, ((0, 0), (half, half))), grad_full)
    glu_part = contract_last(pair_both, normed_half)
    glu_part = jnp.concatenate([glu_part[: 2 * rows], glu_part[2 * rows :]], axis=1)
    early = jnp.concatenate([proj_part, glu_part])
    kernel_part = taps_grad(grad_wide, widened, taps, frames)
    for bit in (1, parts // 2):
        keep, send = halves(early, bit)
        early = keep + swap_bit(send.astype(bf16), bit).astype(f32)
    normed_rows, early = lax.optimization_barrier((normed_rows, early))
    columns = [
        [x * (parts // 2) + 2 * y + core for y in range(parts // 4)]
        for x in range(2)
        for core in range(2)
    ]
    early = lax.all_gather(early.astype(bf16), "seq", axis=0, axis_index_groups=columns)

    line_sums = normed_rows[:sum_rows, frames:].reshape(2, frames)
    frame_means = (line_sums + across(line_sums)) / width
    normed_grad = line_gather(normed_rows[:, :frames].astype(bf16))

    branch_part = jnp.dot(proj_turned, swished_pair, preferred_element_type=f32).astype(bf16)
    branch_part = jnp.pad(
        branch_part.reshape(line, rows, frames), ((0, 0), (0, 2 * rows), (0, 0))
    ).reshape(3 * line * rows, frames)
    normed_grad, branch_part = lax.optimization_barrier((normed_grad, branch_part))
    branch = lax.psum_scatter(
        branch_part, "head", scatter_dimension=0, tiled=True, axis_index_groups=line_groups()
    )[:rows]
    output = (hidden.astype(f32) + branch.astype(f32)).astype(bf16)

    normed_grad = normed_grad.astype(f32)
    scaled = normed_grad * side_half(gain_col)
    stream_half = (
        grad_half.astype(f32)
        + frame_rstd
        * (scaled - frame_means[0:1] - standard * frame_means[1:2])
    ).astype(bf16)
    stream_grad = lax.dynamic_slice_in_dim(stream_half, (me % line) * rows, rows)
    context_pair_grad = jnp.dot(out_half, stream_half, preferred_element_type=f32)

    out_part = contract_last(context_pair, stream_half)
    out_sides = jnp.concatenate(
        [
            jnp.where(side == 0, out_part[:rows], out_part[rows:]),
            jnp.where(side == 0, out_part[rows:], out_part[:rows]),
        ]
    ).reshape(parts, 2 * rows // parts, width // 2)
    tap_lanes = jnp.pad(kernel_part, ((0, 0), (0, 32 - taps)))
    tap_lanes = tap_lanes.reshape(parts, 2 * rows // parts, 16)
    late = jnp.pad(
        jnp.concatenate([out_sides, tap_lanes], axis=2), ((0, 0), (0, 0), (0, 112))
    ).astype(bf16)
    early = jnp.sum(early.astype(f32), axis=0).astype(bf16)
    early_other = across(early[:, width // 2 :])
    seq = lax.axis_index("seq")
    first_row = (seq % 2) * (2 * early.shape[0]) + (seq // (parts // 2)) * early.shape[0]
    is_glu = (first_row + jnp.arange(early.shape[0]) >= rows)[:, None]
    early = jnp.where(is_glu, in_order(early[:, : width // 2], early_other, 1), early)
    piece = jnp.sum(exchange(late, "seq").astype(f32), axis=0).astype(bf16)
    piece, early = lax.optimization_barrier((piece, early))
    early = joined(early, swap_bit(early, parts // 2), parts // 2)
    early = joined(early, swap_bit(early, 1), 1)
    context_send = context_pair_grad[rows:].astype(bf16)
    context_send, early = lax.optimization_barrier((context_send, early))
    context_grad = (context_pair_grad[:rows] + across(context_send).astype(f32)).astype(bf16)
    early = early.astype(f32).reshape(3, rows, width)
    stays = (lax.axis_index("seq") // (parts // 2)) == side
    moves = [
        (h * parts + s, (h + line) % heads * parts + (s + parts // 2) % parts)
        for h in range(heads)
        for s in range(parts)
        if s // (parts // 2) != h // line
    ]
    moved = lax.ppermute(piece, ("head", "seq"), moves)
    out_lanes = lax.broadcasted_iota(jnp.int32, piece.shape, 1) < width // 2
    piece = jnp.where(out_lanes & ~stays, moved, piece)
    late = gather(piece, "seq")
    out_weight_grad = (
        jnp.swapaxes(late[:, :, : width // 2].reshape(2, rows, width // 2), 0, 1)
        .reshape(rows, width)
        .astype(f32)
    )
    kernel_grad = late[:, :, width // 2 : width // 2 + 16].reshape(rows, 32)[:, :taps].astype(f32)
    return (
        output,
        stream_grad,
        context_grad,
        out_weight_grad,
        early[1:],
        kernel_grad,
        gain_total,
        bias_total,
        early[0],
    )


def solution(mesh):
    return jax.shard_map(
        on_device,
        mesh=mesh,
        in_specs=(
            P("head", "seq"),
            P("head", "seq"),
            P("head", None),
            P(),
            P(),
            P(None, "head", None),
            P("head", None),
            P("head"),
            P("head"),
            P("head", None),
            P("head", "seq"),
        ),
        out_specs=(
            P("head", "seq"),
            P("head", "seq"),
            P("head", "seq"),
            P("head", None),
            P(None, "head", None),
            P("head", None),
            P("head"),
            P("head"),
            P("head", None),
        ),
        check_vma=False,
    )
```

```python
import functools

import jax
import jax.numpy as jnp
from jax import lax
from jax.experimental import pallas as pl
from jax.experimental.pallas import tpu as pltpu
from jax.sharding import PartitionSpec as P

epsilon = 1e-05
f32 = jnp.float32
bf16 = jnp.bfloat16


def contract_lead(first_op, second_op):
    return lax.dot_general(
        first_op, second_op, (((0,), (0,)), ((), ())), preferred_element_type=f32
    )


def contract_last(first_op, second_op):
    return lax.dot_general(
        first_op, second_op, (((1,), (1,)), ((), ())), preferred_element_type=f32
    )


def exchange(blocks, axis):
    return lax.all_to_all(blocks, axis, 0, 0, tiled=True)


def gather(block, axis):
    count = lax.axis_size(axis)
    copies = jnp.broadcast_to(block[None], (count, *block.shape))
    return exchange(copies, axis)


def line_groups():
    half = lax.axis_size("head") // 2
    return [[side * half + i for i in range(half)] for side in range(2)]


def across(operand):
    count = lax.axis_size("head")
    return lax.ppermute(operand, "head", [(i, (i + count // 2) % count) for i in range(count)])


def swap_bit(operand, bit):
    count = lax.axis_size("seq")
    return lax.ppermute(operand, "seq", [(i, i ^ bit) for i in range(count)])


def halves(operand, bit):
    mine = (lax.axis_index("seq") // bit) % 2
    size = operand.shape[0] // 2
    keep = lax.dynamic_slice_in_dim(operand, mine * size, size)
    send = lax.dynamic_slice_in_dim(operand, (1 - mine) * size, size)
    return keep, send


def joined(mine_rows, other_rows, bit):
    low = (lax.axis_index("seq") // bit) % 2 == 0
    return jnp.concatenate(
        [jnp.where(low, mine_rows, other_rows), jnp.where(low, other_rows, mine_rows)]
    )


def shifted_left(operand, distance):
    lanes = operand.shape[1]
    return pltpu.roll(operand, (lanes - distance) % lanes, 1)


def conv_back_kernel(
    consts_ref, taps_ref, inside_ref, swish_ref, conv_ref, pair_out_ref, pair_ref, grad_ref, *, taps
):
    frames = pair_ref.shape[2]

    def chunk(index, carry):
        at = pl.ds(pl.multiple_of(index * 16, 16), 16)
        consts = consts_ref[at, :]
        mean, rstd, gain, bias = (consts[:, i : i + 1] for i in range(4))
        bias_mean, gain_mean = consts[:, 4:5], consts[:, 5:6]
        unit = (conv_ref[at, :] - mean) * rstd
        shifted = unit * gain + bias
        sig = jax.nn.sigmoid(shifted)
        shift_grad = swish_ref[at, :] * sig * (1.0 + shifted * (1.0 - sig))
        grad = rstd * gain * (shift_grad - bias_mean - unit * gain_mean)
        grad = jnp.where(inside_ref[...] > 0.0, grad, 0.0).astype(bf16).astype(f32)
        grad_ref[at, :] = grad
        kernel = taps_ref[at, :]
        total = kernel[:, 0:1] * shifted_left(grad, taps - 1)[:, :frames]
        for tap in range(1, taps):
            total = total + kernel[:, tap : tap + 1] * shifted_left(grad, taps - 1 - tap)[:, :frames]
        gate_sig = jax.nn.sigmoid(pair_out_ref[1, at, :])
        value_grad = total * gate_sig
        pair_ref[0, at, :] = value_grad.astype(bf16)
        pair_ref[1, at, :] = (value_grad * pair_out_ref[0, at, :] * (1.0 - gate_sig)).astype(bf16)
        return carry

    lax.fori_loop(0, pair_ref.shape[1] // 16, chunk, 0)


def line_product_kernel(weight_ref, operand_ref, extra_ref, out_ref):
    lines, rows, lanes = out_ref.shape
    frames = operand_ref.shape[1]
    product = jnp.dot(weight_ref[...], operand_ref[...], preferred_element_type=f32).astype(bf16)
    for index in range(lines):
        out_ref[index, :, :frames] = product[index * rows : (index + 1) * rows]
        out_ref[index, :, frames:lanes] = extra_ref[...]


def line_product(weight, operand, extra, lines):
    rows, lanes = extra.shape[0], operand.shape[1] + extra.shape[1]
    return pl.pallas_call(
        line_product_kernel,
        out_shape=jax.ShapeDtypeStruct((lines, rows, lanes), bf16),
        compiler_params=pltpu.CompilerParams(vmem_limit_bytes=32 * 1024 * 1024),
        name="line_product",
    )(weight, operand, extra)


def taps_grad_kernel(grad_ref, widened_ref, out_ref, lane_sums, *, taps, frames):
    half = taps // 2
    rows, lanes = grad_ref.shape
    inside = lax.broadcasted_iota(jnp.int32, (16, lanes), 1) < frames

    def chunk(index, carry):
        first = pl.multiple_of(index * 16, 16)
        grad = jnp.where(inside, shifted_left(grad_ref[pl.ds(first, 16), :], half), 0.0)
        widened = widened_ref[pl.ds(first, 16), :].astype(f32)
        for tap in range(taps):
            product = grad * shifted_left(widened, half + tap)
            total = product[:, :128]
            for lane in range(128, lanes, 128):
                total = total + product[:, lane : lane + 128]
            lane_sums[pl.ds(pl.multiple_of(tap * rows + first, 16), 16), :] = total
        return carry

    lax.fori_loop(0, rows // 16, chunk, 0)
    out_ref[...] = lax.dot_general(
        jnp.ones((8, 128), f32),
        lane_sums[...],
        (((1,), (1,)), ((), ())),
        preferred_element_type=f32,
        precision=lax.Precision.HIGHEST,
    )


def conv_back(consts, kernel, inside, swish_wide, conv_wide, pair_out, taps):
    return pl.pallas_call(
        functools.partial(conv_back_kernel, taps=taps),
        out_shape=(
            jax.ShapeDtypeStruct(pair_out.shape, bf16),
            jax.ShapeDtypeStruct(conv_wide.shape, f32),
        ),
        name="conv_back",
    )(consts, kernel, inside, swish_wide, conv_wide, pair_out)


def taps_grad(grad_wide, widened, taps, frames):
    rows = grad_wide.shape[0]
    sums = pl.pallas_call(
        functools.partial(taps_grad_kernel, taps=taps, frames=frames),
        out_shape=jax.ShapeDtypeStruct((8, taps * rows), f32),
        scratch_shapes=[pltpu.VMEM((taps * rows, 128), f32)],
        name="taps_grad",
    )(grad_wide, widened)
    return sums[0].reshape(taps, rows).T


def neighbours(operand, half_width):
    count, length = lax.axis_size("seq"), operand.shape[1]
    up = [(i, (i + 1) % count) for i in range(count - 1)]
    down = [(j, i) for i, j in up]
    before = lax.ppermute(operand[:, length - half_width :], "seq", up)
    after = lax.ppermute(operand[:, :half_width], "seq", down)
    return jnp.concatenate([before, operand, after], axis=1)


def on_device(
    context,
    stream,
    out_weight,
    ln_gain,
    ln_bias,
    glu_weight,
    depth_kernel,
    bn_gain,
    bn_bias,
    proj_weight,
    out_grad,
):
    rows, frames = stream.shape
    width = ln_gain.shape[0]
    heads = lax.axis_size("head")
    parts = lax.axis_size("seq")
    frames_all = frames * parts
    taps = depth_kernel.shape[1]
    half = taps // 2
    lanes = -(-(frames + 4 * half) // 128) * 128
    me = lax.axis_index("head")
    line = heads // 2
    side = me // line
    gain_col = ln_gain[:, None]
    bias_col = ln_bias[:, None]

    def own_half(weight):
        keep = lax.dynamic_slice_in_dim(weight, side * (width // 2), width // 2, axis=1)
        send = lax.dynamic_slice_in_dim(weight, (1 - side) * (width // 2), width // 2, axis=1)
        return keep, across(send)

    def line_exchange(blocks):
        blocks = lax.all_to_all(
            blocks,
            "head",
            0,
            0,
            tiled=True,
            axis_index_groups=line_groups(),
        )
        return jnp.sum(blocks.astype(f32), axis=0)

    def line_gather(block):
        blocks = lax.all_to_all(
            jnp.broadcast_to(block[None], (line, *block.shape)),
            "head",
            0,
            0,
            tiled=True,
            axis_index_groups=line_groups(),
        )
        return blocks.reshape(line * block.shape[0], *block.shape[1:])

    out_keep = lax.dynamic_slice_in_dim(out_weight, side * (width // 2), width // 2, axis=1)
    out_send = lax.dynamic_slice_in_dim(out_weight, (1 - side) * (width // 2), width // 2, axis=1)
    swapped = across(jnp.concatenate([context, out_send], axis=1))
    context_pair = jnp.concatenate([context, swapped[:, :frames]])
    out_half = jnp.concatenate([out_keep, swapped[:, frames:]])
    attention = line_exchange(
        contract_lead(out_half, context_pair).astype(bf16).reshape(line, rows, frames)
    )
    hidden = (stream.astype(f32) + attention).astype(bf16)

    glu_half = jnp.concatenate(own_half(glu_weight.reshape(2 * rows, width)))
    proj_half = jnp.concatenate(own_half(proj_weight))
    glu_turned, proj_turned = lax.optimization_barrier((glu_half.T, proj_half.T))

    frames_wide = frames + 2 * half
    grad_mine = neighbours(out_grad, half)
    grad_other = across(grad_mine)
    grad_pair = jnp.stack(
        [jnp.where(side == 0, grad_mine, grad_other), jnp.where(side == 0, grad_other, grad_mine)]
    )
    hidden, _ = lax.optimization_barrier((hidden, grad_pair))
    grad_lines = lax.all_gather(
        grad_pair, "head", axis=1, tiled=False, axis_index_groups=line_groups()
    )

    def side_half(array):
        return lax.dynamic_slice_in_dim(array, side * (width // 2), width // 2)

    def in_order(mine, other, axis):
        return jnp.concatenate(
            [jnp.where(side == 0, mine, other), jnp.where(side == 0, other, mine)], axis=axis
        )

    glu_own = glu_weight.astype(f32)
    gain_outs = jnp.einsum("jcsd,sd->sjc", glu_own.reshape(2, rows, 2, -1), ln_gain.reshape(2, -1))
    gain_gap = jnp.where(side == 0, gain_outs[0] - gain_outs[1], gain_outs[1] - gain_outs[0])
    gain_out = gain_outs[0] + gain_outs[1]
    bias_out = jnp.einsum("jcd,d->jc", glu_own, ln_bias)

    hidden_half = line_gather(hidden)
    half_float = hidden_half.astype(f32)
    half_mean = jnp.mean(half_float, axis=0, keepdims=True)
    half_cent = half_float - half_mean
    half_square = jnp.sum(half_cent * half_cent, axis=0, keepdims=True)
    half_moments = jnp.concatenate([half_mean, half_square])
    gained = (half_cent * side_half(gain_col)).astype(bf16)
    products = jnp.dot(glu_half, gained, preferred_element_type=f32)
    products_send, half_moments = lax.optimization_barrier(
        (products[2 * rows :].astype(bf16), half_moments)
    )
    other_products = across(products_send).astype(f32)
    other_moments = across(half_moments)
    mean_gap = 0.5 * (half_moments[0:1] - other_moments[0:1])
    frame_mean = half_moments[0:1] - mean_gap
    frame_var = (
        half_moments[1:2] + other_moments[1:2] + width * mean_gap * mean_gap
    ) / width
    frame_rstd = lax.rsqrt(frame_var + epsilon)
    products = (products[: 2 * rows] + other_products).reshape(2, rows, frames)
    pair_out = (
        frame_rstd * (products + mean_gap * gain_gap[:, :, None]) + bias_out[:, :, None]
    )
    glu_value, glu_gate = pair_out[0], pair_out[1]
    gate_sig = jax.nn.sigmoid(glu_gate)
    gated_out = (glu_value * gate_sig).astype(bf16)
    widened = neighbours(gated_out, 2 * half)
    widened = jnp.pad(widened, ((0, 0), (0, lanes - widened.shape[1])))
    widened = widened.astype(f32)
    conv_wide = depth_kernel[:, 0:1] * widened[:, 0:frames_wide]
    for tap in range(1, taps):
        conv_wide = (
            conv_wide + depth_kernel[:, tap : tap + 1] * widened[:, tap : tap + frames_wide]
        )

    place = lax.axis_index("seq") * frames - half + jnp.arange(lanes)
    inside = (place >= 0) & (place < frames_all) & (jnp.arange(lanes) < frames_wide)
    inside = inside.astype(f32)[None, :]
    conv_wide = jnp.pad(conv_wide, ((0, 0), (0, lanes - frames_wide)))
    conv_out = conv_wide[:, half : half + frames]
    block_mean = jnp.mean(conv_out, axis=1)
    block_cent = conv_out - block_mean[:, None]
    block_square = jnp.sum(block_cent * block_cent, axis=1)
    moments = gather(jnp.stack([block_mean, block_square]), "seq")
    moments, grad_lines = lax.optimization_barrier((moments, grad_lines))
    grad_full = grad_lines.reshape(width, frames_wide)
    swish_wide = jnp.dot(proj_weight, grad_full, preferred_element_type=f32)
    swish_grad = swish_wide[:, half : half + frames]
    swish_wide = jnp.pad(swish_wide, ((0, 0), (0, lanes - frames_wide)))
    grad_half = lax.dynamic_index_in_dim(grad_lines, side, 0, keepdims=False)
    grad_half = grad_half.reshape(width // 2, frames_wide)[:, half : half + frames]
    chan_mean = jnp.mean(moments[:, 0], axis=0)
    mean_gap = moments[:, 0] - chan_mean
    chan_var = (
        jnp.sum(moments[:, 1], axis=0) + frames * jnp.sum(mean_gap * mean_gap, axis=0)
    ) / frames_all
    chan_rstd = lax.rsqrt(chan_var + epsilon)
    chan_unit = (conv_out - chan_mean[:, None]) * chan_rstd[:, None]
    shifted = chan_unit * bn_gain[:, None] + bn_bias[:, None]
    shift_sig = jax.nn.sigmoid(shifted)
    swished = (shifted * shift_sig).astype(bf16)
    shift_grad = swish_grad * shift_sig * (1.0 + shifted * (1.0 - shift_sig))

    sums = gather(
        jnp.stack([jnp.sum(shift_grad, axis=1), jnp.sum(shift_grad * chan_unit, axis=1)]), "seq"
    )
    bias_total, gain_total = jnp.sum(sums[:, 0], axis=0), jnp.sum(sums[:, 1], axis=0)
    consts = jnp.stack(
        [
            chan_mean,
            chan_rstd,
            bn_gain,
            bn_bias,
            bias_total / frames_all,
            gain_total / frames_all,
        ],
        axis=1,
    )
    pair_grad, grad_wide = conv_back(
        consts, depth_kernel, inside, swish_wide, conv_wide, pair_out, taps
    )

    pair_rows = pair_grad.reshape(2 * rows, frames)
    other_rows = across(jnp.concatenate([pair_rows, swished]))
    pair_both = jnp.concatenate([pair_rows, other_rows[: 2 * rows]])
    swished_pair = jnp.concatenate([swished, other_rows[2 * rows :]])
    pair_float = pair_grad.astype(f32)
    frame_sums = jnp.stack(
        [
            jnp.sum(pair_float * gain_out[:, :, None], axis=(0, 1)),
            jnp.sum(pair_float * (pair_out - bias_out[:, :, None]), axis=(0, 1)),
        ]
    )
    spare = lanes - frames
    sum_rows = 2 * frames // spare
    frame_sums = jnp.pad(
        frame_sums.astype(bf16).reshape(sum_rows, spare), ((0, rows - sum_rows), (0, 0))
    )
    normed_rows = line_exchange(line_product(glu_turned, pair_both, frame_sums, line))

    standard = (half_float - frame_mean) * frame_rstd
    normed_half = (standard * side_half(gain_col) + side_half(bias_col)).astype(bf16)
    proj_part = contract_last(jnp.pad(swished, ((0, 0), (half, half))), grad_full)
    glu_part = contract_last(pair_both, normed_half)
    glu_part = jnp.concatenate([glu_part[: 2 * rows], glu_part[2 * rows :]], axis=1)
    early = jnp.concatenate([proj_part, glu_part])
    kernel_part = taps_grad(grad_wide, widened, taps, frames)
    for bit in (1, parts // 2):
        keep, send = halves(early, bit)
        early = keep + swap_bit(send.astype(bf16), bit).astype(f32)
    normed_rows, early = lax.optimization_barrier((normed_rows, early))
    columns = [
        [x * (parts // 2) + 2 * y + core for y in range(parts // 4)]
        for x in range(2)
        for core in range(2)
    ]
    early = lax.all_gather(early.astype(bf16), "seq", axis=0, axis_index_groups=columns)

    line_sums = normed_rows[:sum_rows, frames:].reshape(2, frames)
    frame_means = (line_sums + across(line_sums)) / width
    normed_grad = line_gather(normed_rows[:, :frames].astype(bf16))

    branch_part = jnp.dot(proj_turned, swished_pair, preferred_element_type=f32).astype(bf16)
    branch_part = jnp.pad(
        branch_part.reshape(line, rows, frames), ((0, 0), (0, 2 * rows), (0, 0))
    ).reshape(3 * line * rows, frames)
    normed_grad, branch_part = lax.optimization_barrier((normed_grad, branch_part))
    branch = lax.psum_scatter(
        branch_part, "head", scatter_dimension=0, tiled=True, axis_index_groups=line_groups()
    )[:rows]
    output = (hidden.astype(f32) + branch.astype(f32)).astype(bf16)

    normed_grad = normed_grad.astype(f32)
    scaled = normed_grad * side_half(gain_col)
    stream_half = (
        grad_half.astype(f32)
        + frame_rstd
        * (scaled - frame_means[0:1] - standard * frame_means[1:2])
    ).astype(bf16)
    stream_grad = lax.dynamic_slice_in_dim(stream_half, (me % line) * rows, rows)
    context_pair_grad = jnp.dot(out_half, stream_half, preferred_element_type=f32)

    out_part = contract_last(context_pair, stream_half)
    out_sides = jnp.concatenate(
        [
            jnp.where(side == 0, out_part[:rows], out_part[rows:]),
            jnp.where(side == 0, out_part[rows:], out_part[:rows]),
        ]
    ).reshape(parts, 2 * rows // parts, width // 2)
    tap_lanes = jnp.pad(kernel_part, ((0, 0), (0, 32 - taps)))
    tap_lanes = tap_lanes.reshape(parts, 2 * rows // parts, 16)
    late = jnp.pad(
        jnp.concatenate([out_sides, tap_lanes], axis=2), ((0, 0), (0, 0), (0, 112))
    ).astype(bf16)
    early = jnp.sum(early.astype(f32), axis=0).astype(bf16)
    early_other = across(early[:, width // 2 :])
    seq = lax.axis_index("seq")
    first_row = (seq % 2) * (2 * early.shape[0]) + (seq // (parts // 2)) * early.shape[0]
    is_glu = (first_row + jnp.arange(early.shape[0]) >= rows)[:, None]
    early = jnp.where(is_glu, in_order(early[:, : width // 2], early_other, 1), early)
    piece = jnp.sum(exchange(late, "seq").astype(f32), axis=0).astype(bf16)
    piece, early = lax.optimization_barrier((piece, early))
    early = joined(early, swap_bit(early, parts // 2), parts // 2)
    stays = (lax.axis_index("seq") // (parts // 2)) == side
    moves = [
        (h * parts + s, (h + line) % heads * parts + (s + parts // 2) % parts)
        for h in range(heads)
        for s in range(parts)
        if s // (parts // 2) != h // line
    ]
    moved = lax.ppermute(piece, ("head", "seq"), moves)
    moved, early = lax.optimization_barrier((moved, early))
    early = joined(early, swap_bit(early, 1), 1)
    context_send = context_pair_grad[rows:].astype(bf16)
    context_send, early = lax.optimization_barrier((context_send, early))
    context_grad = (context_pair_grad[:rows] + across(context_send).astype(f32)).astype(bf16)
    early = early.astype(f32).reshape(3, rows, width)
    out_lanes = lax.broadcasted_iota(jnp.int32, piece.shape, 1) < width // 2
    piece = jnp.where(out_lanes & ~stays, moved, piece)
    late = gather(piece, "seq")
    out_weight_grad = (
        jnp.swapaxes(late[:, :, : width // 2].reshape(2, rows, width // 2), 0, 1)
        .reshape(rows, width)
        .astype(f32)
    )
    kernel_grad = late[:, :, width // 2 : width // 2 + 16].reshape(rows, 32)[:, :taps].astype(f32)
    return (
        output,
        stream_grad,
        context_grad,
        out_weight_grad,
        early[1:],
        kernel_grad,
        gain_total,
        bias_total,
        early[0],
    )


def solution(mesh):
    return jax.shard_map(
        on_device,
        mesh=mesh,
        in_specs=(
            P("head", "seq"),
            P("head", "seq"),
            P("head", None),
            P(),
            P(),
            P(None, "head", None),
            P("head", None),
            P("head"),
            P("head"),
            P("head", None),
            P("head", "seq"),
        ),
        out_specs=(
            P("head", "seq"),
            P("head", "seq"),
            P("head", "seq"),
            P("head", None),
            P(None, "head", None),
            P("head", None),
            P("head"),
            P("head"),
            P("head", None),
        ),
        check_vma=False,
    )
```

```python
import functools

import jax
import jax.numpy as jnp
from jax import lax
from jax.experimental import pallas as pl
from jax.experimental.pallas import tpu as pltpu
from jax.sharding import PartitionSpec as P

epsilon = 1e-05
f32 = jnp.float32
bf16 = jnp.bfloat16


def contract_lead(first_op, second_op):
    return lax.dot_general(
        first_op, second_op, (((0,), (0,)), ((), ())), preferred_element_type=f32
    )


def contract_last(first_op, second_op):
    return lax.dot_general(
        first_op, second_op, (((1,), (1,)), ((), ())), preferred_element_type=f32
    )


def exchange(blocks, axis):
    return lax.all_to_all(blocks, axis, 0, 0, tiled=True)


def gather(block, axis):
    count = lax.axis_size(axis)
    copies = jnp.broadcast_to(block[None], (count, *block.shape))
    return exchange(copies, axis)


def line_groups():
    half = lax.axis_size("head") // 2
    return [[side * half + i for i in range(half)] for side in range(2)]


def across(operand):
    count = lax.axis_size("head")
    return lax.ppermute(operand, "head", [(i, (i + count // 2) % count) for i in range(count)])


def swap_bit(operand, bit):
    count = lax.axis_size("seq")
    return lax.ppermute(operand, "seq", [(i, i ^ bit) for i in range(count)])


def halves(operand, bit):
    mine = (lax.axis_index("seq") // bit) % 2
    size = operand.shape[0] // 2
    keep = lax.dynamic_slice_in_dim(operand, mine * size, size)
    send = lax.dynamic_slice_in_dim(operand, (1 - mine) * size, size)
    return keep, send


def joined(mine_rows, other_rows, bit):
    low = (lax.axis_index("seq") // bit) % 2 == 0
    return jnp.concatenate(
        [jnp.where(low, mine_rows, other_rows), jnp.where(low, other_rows, mine_rows)]
    )


def shifted_left(operand, distance):
    lanes = operand.shape[1]
    return pltpu.roll(operand, (lanes - distance) % lanes, 1)


def conv_back_kernel(
    consts_ref, taps_ref, inside_ref, swish_ref, conv_ref, pair_out_ref, pair_ref, grad_ref, *, taps
):
    frames = pair_ref.shape[2]

    def chunk(index, carry):
        at = pl.ds(pl.multiple_of(index * 16, 16), 16)
        consts = consts_ref[at, :]
        mean, rstd, gain, bias = (consts[:, i : i + 1] for i in range(4))
        bias_mean, gain_mean = consts[:, 4:5], consts[:, 5:6]
        unit = (conv_ref[at, :] - mean) * rstd
        shifted = unit * gain + bias
        sig = jax.nn.sigmoid(shifted)
        shift_grad = swish_ref[at, :] * sig * (1.0 + shifted * (1.0 - sig))
        grad = rstd * gain * (shift_grad - bias_mean - unit * gain_mean)
        grad = jnp.where(inside_ref[...] > 0.0, grad, 0.0).astype(bf16).astype(f32)
        grad_ref[at, :] = grad
        kernel = taps_ref[at, :]
        total = kernel[:, 0:1] * shifted_left(grad, taps - 1)[:, :frames]
        for tap in range(1, taps):
            total = total + kernel[:, tap : tap + 1] * shifted_left(grad, taps - 1 - tap)[:, :frames]
        gate_sig = jax.nn.sigmoid(pair_out_ref[1, at, :])
        value_grad = total * gate_sig
        pair_ref[0, at, :] = value_grad.astype(bf16)
        pair_ref[1, at, :] = (value_grad * pair_out_ref[0, at, :] * (1.0 - gate_sig)).astype(bf16)
        return carry

    lax.fori_loop(0, pair_ref.shape[1] // 16, chunk, 0)


def line_product_kernel(weight_ref, operand_ref, extra_ref, out_ref):
    lines, rows, lanes = out_ref.shape
    frames = operand_ref.shape[1]
    product = jnp.dot(weight_ref[...], operand_ref[...], preferred_element_type=f32).astype(bf16)
    for index in range(lines):
        out_ref[index, :, :frames] = product[index * rows : (index + 1) * rows]
        out_ref[index, :, frames:lanes] = extra_ref[...]


def line_product(weight, operand, extra, lines):
    rows, lanes = extra.shape[0], operand.shape[1] + extra.shape[1]
    return pl.pallas_call(
        line_product_kernel,
        out_shape=jax.ShapeDtypeStruct((lines, rows, lanes), bf16),
        compiler_params=pltpu.CompilerParams(vmem_limit_bytes=32 * 1024 * 1024),
        name="line_product",
    )(weight, operand, extra)


def taps_grad_kernel(grad_ref, widened_ref, out_ref, lane_sums, *, taps, frames):
    half = taps // 2
    rows, lanes = grad_ref.shape
    inside = lax.broadcasted_iota(jnp.int32, (16, lanes), 1) < frames

    def chunk(index, carry):
        first = pl.multiple_of(index * 16, 16)
        grad = jnp.where(inside, shifted_left(grad_ref[pl.ds(first, 16), :], half), 0.0)
        widened = widened_ref[pl.ds(first, 16), :].astype(f32)
        for tap in range(taps):
            product = grad * shifted_left(widened, half + tap)
            total = product[:, :128]
            for lane in range(128, lanes, 128):
                total = total + product[:, lane : lane + 128]
            lane_sums[pl.ds(pl.multiple_of(tap * rows + first, 16), 16), :] = total
        return carry

    lax.fori_loop(0, rows // 16, chunk, 0)
    out_ref[...] = lax.dot_general(
        jnp.ones((8, 128), f32),
        lane_sums[...],
        (((1,), (1,)), ((), ())),
        preferred_element_type=f32,
        precision=lax.Precision.HIGHEST,
    )


def conv_back(consts, kernel, inside, swish_wide, conv_wide, pair_out, taps):
    return pl.pallas_call(
        functools.partial(conv_back_kernel, taps=taps),
        out_shape=(
            jax.ShapeDtypeStruct(pair_out.shape, bf16),
            jax.ShapeDtypeStruct(conv_wide.shape, f32),
        ),
        name="conv_back",
    )(consts, kernel, inside, swish_wide, conv_wide, pair_out)


def taps_grad(grad_wide, widened, taps, frames):
    rows = grad_wide.shape[0]
    sums = pl.pallas_call(
        functools.partial(taps_grad_kernel, taps=taps, frames=frames),
        out_shape=jax.ShapeDtypeStruct((8, taps * rows), f32),
        scratch_shapes=[pltpu.VMEM((taps * rows, 128), f32)],
        name="taps_grad",
    )(grad_wide, widened)
    return sums[0].reshape(taps, rows).T


def neighbours(operand, half_width):
    count, length = lax.axis_size("seq"), operand.shape[1]
    up = [(i, (i + 1) % count) for i in range(count - 1)]
    down = [(j, i) for i, j in up]
    before = lax.ppermute(operand[:, length - half_width :], "seq", up)
    after = lax.ppermute(operand[:, :half_width], "seq", down)
    return jnp.concatenate([before, operand, after], axis=1)


def on_device(
    context,
    stream,
    out_weight,
    ln_gain,
    ln_bias,
    glu_weight,
    depth_kernel,
    bn_gain,
    bn_bias,
    proj_weight,
    out_grad,
):
    rows, frames = stream.shape
    width = ln_gain.shape[0]
    heads = lax.axis_size("head")
    parts = lax.axis_size("seq")
    frames_all = frames * parts
    taps = depth_kernel.shape[1]
    half = taps // 2
    lanes = -(-(frames + 4 * half) // 128) * 128
    me = lax.axis_index("head")
    line = heads // 2
    side = me // line
    gain_col = ln_gain[:, None]
    bias_col = ln_bias[:, None]

    def own_half(weight):
        keep = lax.dynamic_slice_in_dim(weight, side * (width // 2), width // 2, axis=1)
        send = lax.dynamic_slice_in_dim(weight, (1 - side) * (width // 2), width // 2, axis=1)
        return keep, across(send)

    def line_exchange(blocks):
        blocks = lax.all_to_all(
            blocks,
            "head",
            0,
            0,
            tiled=True,
            axis_index_groups=line_groups(),
        )
        return jnp.sum(blocks.astype(f32), axis=0)

    def line_gather(block):
        blocks = lax.all_to_all(
            jnp.broadcast_to(block[None], (line, *block.shape)),
            "head",
            0,
            0,
            tiled=True,
            axis_index_groups=line_groups(),
        )
        return blocks.reshape(line * block.shape[0], *block.shape[1:])

    out_keep = lax.dynamic_slice_in_dim(out_weight, side * (width // 2), width // 2, axis=1)
    out_send = lax.dynamic_slice_in_dim(out_weight, (1 - side) * (width // 2), width // 2, axis=1)
    swapped = across(jnp.concatenate([context, out_send], axis=1))
    context_pair = jnp.concatenate([context, swapped[:, :frames]])
    out_half = jnp.concatenate([out_keep, swapped[:, frames:]])
    attention = line_exchange(
        contract_lead(out_half, context_pair).astype(bf16).reshape(line, rows, frames)
    )
    hidden = (stream.astype(f32) + attention).astype(bf16)

    glu_half = jnp.concatenate(own_half(glu_weight.reshape(2 * rows, width)))
    proj_half = jnp.concatenate(own_half(proj_weight))
    glu_turned, proj_turned = lax.optimization_barrier((glu_half.T, proj_half.T))

    frames_wide = frames + 2 * half
    grad_mine = neighbours(out_grad, half)
    grad_other = across(grad_mine)
    grad_pair = jnp.stack(
        [jnp.where(side == 0, grad_mine, grad_other), jnp.where(side == 0, grad_other, grad_mine)]
    )
    hidden, _ = lax.optimization_barrier((hidden, grad_pair))
    grad_lines = lax.all_gather(
        grad_pair, "head", axis=1, tiled=False, axis_index_groups=line_groups()
    )

    def side_half(array):
        return lax.dynamic_slice_in_dim(array, side * (width // 2), width // 2)

    def in_order(mine, other, axis):
        return jnp.concatenate(
            [jnp.where(side == 0, mine, other), jnp.where(side == 0, other, mine)], axis=axis
        )

    glu_own = glu_weight.astype(f32)
    gain_outs = jnp.einsum("jcsd,sd->sjc", glu_own.reshape(2, rows, 2, -1), ln_gain.reshape(2, -1))
    gain_gap = jnp.where(side == 0, gain_outs[0] - gain_outs[1], gain_outs[1] - gain_outs[0])
    gain_out = gain_outs[0] + gain_outs[1]
    bias_out = jnp.einsum("jcd,d->jc", glu_own, ln_bias)

    hidden_half = line_gather(hidden)
    half_float = hidden_half.astype(f32)
    half_mean = jnp.mean(half_float, axis=0, keepdims=True)
    half_cent = half_float - half_mean
    half_square = jnp.sum(half_cent * half_cent, axis=0, keepdims=True)
    half_moments = jnp.concatenate([half_mean, half_square])
    gained = (half_cent * side_half(gain_col)).astype(bf16)
    products = jnp.dot(glu_half, gained, preferred_element_type=f32)
    products_send, half_moments = lax.optimization_barrier(
        (products[2 * rows :].astype(bf16), half_moments)
    )
    other_products = across(products_send).astype(f32)
    other_moments = across(half_moments)
    mean_gap = 0.5 * (half_moments[0:1] - other_moments[0:1])
    frame_mean = half_moments[0:1] - mean_gap
    frame_var = (
        half_moments[1:2] + other_moments[1:2] + width * mean_gap * mean_gap
    ) / width
    frame_rstd = lax.rsqrt(frame_var + epsilon)
    products = (products[: 2 * rows] + other_products).reshape(2, rows, frames)
    pair_out = (
        frame_rstd * (products + mean_gap * gain_gap[:, :, None]) + bias_out[:, :, None]
    )
    glu_value, glu_gate = pair_out[0], pair_out[1]
    gate_sig = jax.nn.sigmoid(glu_gate)
    gated_out = (glu_value * gate_sig).astype(bf16)
    widened = neighbours(gated_out, 2 * half)
    widened = jnp.pad(widened, ((0, 0), (0, lanes - widened.shape[1])))
    widened = widened.astype(f32)
    conv_wide = depth_kernel[:, 0:1] * widened[:, 0:frames_wide]
    for tap in range(1, taps):
        conv_wide = (
            conv_wide + depth_kernel[:, tap : tap + 1] * widened[:, tap : tap + frames_wide]
        )

    place = lax.axis_index("seq") * frames - half + jnp.arange(lanes)
    inside = (place >= 0) & (place < frames_all) & (jnp.arange(lanes) < frames_wide)
    inside = inside.astype(f32)[None, :]
    conv_wide = jnp.pad(conv_wide, ((0, 0), (0, lanes - frames_wide)))
    conv_out = conv_wide[:, half : half + frames]
    block_mean = jnp.mean(conv_out, axis=1)
    block_cent = conv_out - block_mean[:, None]
    block_square = jnp.sum(block_cent * block_cent, axis=1)
    moments = gather(jnp.stack([block_mean, block_square]), "seq")
    moments, grad_lines = lax.optimization_barrier((moments, grad_lines))
    grad_full = grad_lines.reshape(width, frames_wide)
    swish_wide = jnp.dot(proj_weight, grad_full, preferred_element_type=f32)
    swish_grad = swish_wide[:, half : half + frames]
    swish_wide = jnp.pad(swish_wide, ((0, 0), (0, lanes - frames_wide)))
    grad_half = lax.dynamic_index_in_dim(grad_lines, side, 0, keepdims=False)
    grad_half = grad_half.reshape(width // 2, frames_wide)[:, half : half + frames]
    chan_mean = jnp.mean(moments[:, 0], axis=0)
    mean_gap = moments[:, 0] - chan_mean
    chan_var = (
        jnp.sum(moments[:, 1], axis=0) + frames * jnp.sum(mean_gap * mean_gap, axis=0)
    ) / frames_all
    chan_rstd = lax.rsqrt(chan_var + epsilon)
    chan_unit = (conv_out - chan_mean[:, None]) * chan_rstd[:, None]
    shifted = chan_unit * bn_gain[:, None] + bn_bias[:, None]
    shift_sig = jax.nn.sigmoid(shifted)
    swished = (shifted * shift_sig).astype(bf16)
    shift_grad = swish_grad * shift_sig * (1.0 + shifted * (1.0 - shift_sig))

    sums = gather(
        jnp.stack([jnp.sum(shift_grad, axis=1), jnp.sum(shift_grad * chan_unit, axis=1)]), "seq"
    )
    bias_total, gain_total = jnp.sum(sums[:, 0], axis=0), jnp.sum(sums[:, 1], axis=0)
    consts = jnp.stack(
        [
            chan_mean,
            chan_rstd,
            bn_gain,
            bn_bias,
            bias_total / frames_all,
            gain_total / frames_all,
        ],
        axis=1,
    )
    pair_grad, grad_wide = conv_back(
        consts, depth_kernel, inside, swish_wide, conv_wide, pair_out, taps
    )

    pair_rows = pair_grad.reshape(2 * rows, frames)
    other_rows = across(jnp.concatenate([pair_rows, swished]))
    pair_both = jnp.concatenate([pair_rows, other_rows[: 2 * rows]])
    swished_pair = jnp.concatenate([swished, other_rows[2 * rows :]])
    pair_float = pair_grad.astype(f32)
    frame_sums = jnp.stack(
        [
            jnp.sum(pair_float * gain_out[:, :, None], axis=(0, 1)),
            jnp.sum(pair_float * (pair_out - bias_out[:, :, None]), axis=(0, 1)),
        ]
    )
    spare = lanes - frames
    sum_rows = 2 * frames // spare
    frame_sums = jnp.pad(
        frame_sums.astype(bf16).reshape(sum_rows, spare), ((0, rows - sum_rows), (0, 0))
    )
    normed_chunks = line_product(glu_turned, pair_both, frame_sums, line)
    normed_chunks, pair_after, swished_after = lax.optimization_barrier(
        (normed_chunks, pair_both, swished)
    )
    normed_rows = line_exchange(normed_chunks)

    standard = (half_float - frame_mean) * frame_rstd
    normed_half = (standard * side_half(gain_col) + side_half(bias_col)).astype(bf16)
    proj_part = contract_last(jnp.pad(swished_after, ((0, 0), (half, half))), grad_full)
    glu_part = contract_last(pair_after, normed_half)
    glu_part = jnp.concatenate([glu_part[: 2 * rows], glu_part[2 * rows :]], axis=1)
    early = jnp.concatenate([proj_part, glu_part])
    kernel_part = taps_grad(grad_wide, widened, taps, frames)
    for bit in (1, parts // 2):
        keep, send = halves(early, bit)
        early = keep + swap_bit(send.astype(bf16), bit).astype(f32)
    normed_rows, early = lax.optimization_barrier((normed_rows, early))
    columns = [
        [x * (parts // 2) + 2 * y + core for y in range(parts // 4)]
        for x in range(2)
        for core in range(2)
    ]
    early = lax.all_gather(early.astype(bf16), "seq", axis=0, axis_index_groups=columns)

    line_sums = normed_rows[:sum_rows, frames:].reshape(2, frames)
    frame_means = (line_sums + across(line_sums)) / width
    normed_grad = line_gather(normed_rows[:, :frames].astype(bf16))

    branch_part = jnp.dot(proj_turned, swished_pair, preferred_element_type=f32).astype(bf16)
    branch_part = jnp.pad(
        branch_part.reshape(line, rows, frames), ((0, 0), (0, 2 * rows), (0, 0))
    ).reshape(3 * line * rows, frames)
    normed_grad, branch_part = lax.optimization_barrier((normed_grad, branch_part))
    branch = lax.psum_scatter(
        branch_part, "head", scatter_dimension=0, tiled=True, axis_index_groups=line_groups()
    )[:rows]
    output = (hidden.astype(f32) + branch.astype(f32)).astype(bf16)

    normed_grad = normed_grad.astype(f32)
    scaled = normed_grad * side_half(gain_col)
    stream_half = (
        grad_half.astype(f32)
        + frame_rstd
        * (scaled - frame_means[0:1] - standard * frame_means[1:2])
    ).astype(bf16)
    stream_grad = lax.dynamic_slice_in_dim(stream_half, (me % line) * rows, rows)
    context_pair_grad = jnp.dot(out_half, stream_half, preferred_element_type=f32)

    out_part = contract_last(context_pair, stream_half)
    out_sides = jnp.concatenate(
        [
            jnp.where(side == 0, out_part[:rows], out_part[rows:]),
            jnp.where(side == 0, out_part[rows:], out_part[:rows]),
        ]
    ).reshape(parts, 2 * rows // parts, width // 2)
    tap_lanes = jnp.pad(kernel_part, ((0, 0), (0, 32 - taps)))
    tap_lanes = tap_lanes.reshape(parts, 2 * rows // parts, 16)
    late = jnp.pad(
        jnp.concatenate([out_sides, tap_lanes], axis=2), ((0, 0), (0, 0), (0, 112))
    ).astype(bf16)
    early = jnp.sum(early.astype(f32), axis=0).astype(bf16)
    early_other = across(early[:, width // 2 :])
    seq = lax.axis_index("seq")
    first_row = (seq % 2) * (2 * early.shape[0]) + (seq // (parts // 2)) * early.shape[0]
    is_glu = (first_row + jnp.arange(early.shape[0]) >= rows)[:, None]
    early = jnp.where(is_glu, in_order(early[:, : width // 2], early_other, 1), early)
    piece = jnp.sum(exchange(late, "seq").astype(f32), axis=0).astype(bf16)
    piece, early = lax.optimization_barrier((piece, early))
    early = joined(early, swap_bit(early, parts // 2), parts // 2)
    stays = (lax.axis_index("seq") // (parts // 2)) == side
    moves = [
        (h * parts + s, (h + line) % heads * parts + (s + parts // 2) % parts)
        for h in range(heads)
        for s in range(parts)
        if s // (parts // 2) != h // line
    ]
    moved = lax.ppermute(piece, ("head", "seq"), moves)
    moved, early = lax.optimization_barrier((moved, early))
    early = joined(early, swap_bit(early, 1), 1)
    context_send = context_pair_grad[rows:].astype(bf16)
    context_send, early = lax.optimization_barrier((context_send, early))
    context_grad = (context_pair_grad[:rows] + across(context_send).astype(f32)).astype(bf16)
    early = early.astype(f32).reshape(3, rows, width)
    out_lanes = lax.broadcasted_iota(jnp.int32, piece.shape, 1) < width // 2
    piece = jnp.where(out_lanes & ~stays, moved, piece)
    late = gather(piece, "seq")
    out_weight_grad = (
        jnp.swapaxes(late[:, :, : width // 2].reshape(2, rows, width // 2), 0, 1)
        .reshape(rows, width)
        .astype(f32)
    )
    kernel_grad = late[:, :, width // 2 : width // 2 + 16].reshape(rows, 32)[:, :taps].astype(f32)
    return (
        output,
        stream_grad,
        context_grad,
        out_weight_grad,
        early[1:],
        kernel_grad,
        gain_total,
        bias_total,
        early[0],
    )


def solution(mesh):
    return jax.shard_map(
        on_device,
        mesh=mesh,
        in_specs=(
            P("head", "seq"),
            P("head", "seq"),
            P("head", None),
            P(),
            P(),
            P(None, "head", None),
            P("head", None),
            P("head"),
            P("head"),
            P("head", None),
            P("head", "seq"),
        ),
        out_specs=(
            P("head", "seq"),
            P("head", "seq"),
            P("head", "seq"),
            P("head", None),
            P(None, "head", None),
            P("head", None),
            P("head"),
            P("head"),
            P("head", None),
        ),
        check_vma=False,
    )
```
